512 devices in a mesh: sib: 32 (over y, x, core), ctx: 8 (over z_lo), tp: 2 (over z_hi).
Axes of the slice: x: 4, y: 4, z: 16 (z_hi: 2, z_lo: 8; z = z_hi * 8 + z_lo), core: 2. Of those that a mesh axis runs over, the one named last changes fastest.
Arguments:
- queries: bfloat16 [32, 4, 1024, 512], P('sib', 'tp', 'ctx'), may hold values from -27 to 27
- output_gradient: bfloat16 [32, 4, 1024, 512], P('sib', 'tp', 'ctx'), may hold values from -6 to 6
- forward_output: bfloat16 [32, 4, 1024, 512], P('sib', 'tp', 'ctx'), may hold values from -6 to 6
- sibling_key_matrix: bfloat16 [32, 1024, 512], P('sib', 'ctx'), may hold values from -6 to 6
- sibling_value_matrix: bfloat16 [32, 1024, 512], P('sib', 'ctx'), may hold values from -6 to 6
- prefix_keys: bfloat16 [1024, 512], P(('sib', 'ctx')), may hold values from -9 to 9
- prefix_value_matrix: bfloat16 [1024, 512], P(('sib', 'ctx')), may hold values from -6 to 6
- lengths: int32 [32], replicated, may hold values from 1 to 1024, 20480 in all
Outputs:
- query_grads: bfloat16 [32, 4, 1024, 512], P('sib', 'tp', 'ctx')
- sibling_key_grads: bfloat16 [32, 1024, 512], P('sib', ('ctx', 'tp'))
- sibling_value_grads: bfloat16 [32, 1024, 512], P('sib', ('ctx', 'tp'))
- prefix_key_grads: bfloat16 [1024, 512], P(('sib', 'ctx', 'tp'))
- prefix_value_grads: bfloat16 [1024, 512], P(('sib', 'ctx', 'tp'))
The draws below stay inside these ranges and needn't reach their ends.
Inputs may be any that keep to these rules, and one draw needn't show every extreme that they name: `lengths`: at least one sibling is full, with 1024 live tokens.
All inputs are finite; a program needn't handle non-finite values.
Results may differ from the reference program's by a relative error of at most 0.015.
Values may be sent and summed in bfloat16 or wider, within the bound.
No kernel may reach another device: no remote copies, remote signals or barrier semaphores. Data moves between devices by JAX's collectives and lax.ppermute only.
A program may use at most 64 MiB of HBM per device.

```python
import math
import jax
import jax.numpy as jnp
import numpy as np
from jax import lax

HEAD_SIZE = 128
KV_HEAD_COUNT = 4
QUERY_PER_KV = 4
R = 128
PS = 4
SIBLING_COUNT = 32
SIBLING_SLOTS = 1024
PREFIX_TOKENS = 1024
N_SIB = 32
N_CTX = 8


def draw_queries(key, part):
    key = jax.random.fold_in(key, 11)
    sampled_arrays = jnp.clip(jax.random.normal(key, (SIBLING_COUNT, QUERY_PER_KV, SIBLING_SLOTS, KV_HEAD_COUNT, HEAD_SIZE), jnp.float32), -4.0, 4.0)
    return sampled_arrays.reshape(SIBLING_COUNT, QUERY_PER_KV, SIBLING_SLOTS, KV_HEAD_COUNT * HEAD_SIZE).astype(jnp.bfloat16)


def draw_prefix_keys(key, part):
    key = jax.random.fold_in(key, 23)
    sampled_arrays = jnp.clip(jax.random.normal(key, (PREFIX_TOKENS, KV_HEAD_COUNT, HEAD_SIZE), jnp.float32), -4.0, 4.0)
    return sampled_arrays.reshape(PREFIX_TOKENS, KV_HEAD_COUNT * HEAD_SIZE).astype(jnp.bfloat16)


def steps_of(stream_key, shape, pieces, smallest, largest):
    loudness, own = 1.0, jax.random.fold_in(stream_key, 6)
    for axis_at, parts in pieces:
        heights = jnp.exp(jax.random.uniform(jax.random.fold_in(own, axis_at), (parts,), jnp.float32, smallest / len(pieces), largest / len(pieces)))
        loudness = loudness * jnp.repeat(heights, shape[axis_at] // parts).reshape([-1 if axis == axis_at else 1 for axis in range(len(shape))])
    return loudness


def profile(number_of, total, most, lean):
    weights = [(1 << 20) // math.isqrt(rank ** lean) + 1 for rank in range(2, number_of + 1)]
    surplus, counts = total - most - (number_of - 1), [1] * (number_of - 1)
    while surplus > 0:
        free = [i for i in range(number_of - 1) if counts[i] < most]
        whole, left = sum([weights[i] for i in free]), surplus
        for i in free:
            extra = min(most - counts[i], max(1, left * weights[i] // whole), surplus)
            counts[i] = counts[i] + extra
            surplus = surplus - extra
    return np.array([most] + counts)


def uneven(key, amount, total, reach, lean):
    if amount == 2:
        one = jax.random.randint(key, (), max(1, total - reach), min(reach, total - 1) + 1)
        return jnp.stack([one, total - one])
    sizes = jnp.asarray(profile(amount, total, reach, lean), jnp.int32)
    twos = (amount - 1) // 2
    giver, sink = sizes[1:1 + 2 * twos:2], sizes[2:2 + 2 * twos:2]
    margin = jnp.minimum(giver - 1, reach - sink)
    shifted = jax.random.randint(jax.random.fold_in(key, 1), (twos,), 0, 1 << 20) % (margin + 1)
    sizes = sizes.at[1:1 + 2 * twos:2].set(giver - shifted).at[2:2 + 2 * twos:2].set(sink + shifted)
    return sizes[jax.random.permutation(jax.random.fold_in(key, 2), amount)]


def noise(stream_key, dims, width, most, pieces=(), kind=jnp.bfloat16):
    level = steps_of(stream_key, dims, pieces, -0.22, 0.18) if pieces else 1.0
    result = jax.random.normal(stream_key, dims, jnp.float32) * width * level
    return jnp.minimum(jnp.maximum(result, -most), most).astype(kind)


def setup_inputs(seed: int = 0) -> dict:
    splits = jax.random.split(jax.random.key(seed), 9)
    return {
        "queries": draw_queries(jax.random.fold_in(splits[8], 71), 0),
        "output_gradient": noise(splits[1], (SIBLING_COUNT, QUERY_PER_KV, SIBLING_SLOTS, KV_HEAD_COUNT * HEAD_SIZE), 1.0, 6.0, ((0, 32), (1, 2), (2, 8))),
        "forward_output": noise(splits[2], (SIBLING_COUNT, QUERY_PER_KV, SIBLING_SLOTS, KV_HEAD_COUNT * HEAD_SIZE), 1.0, 6.0, ((0, 32), (1, 2), (2, 8))),
        "sibling_key_matrix": noise(splits[3], (SIBLING_COUNT, SIBLING_SLOTS, KV_HEAD_COUNT * HEAD_SIZE), 1.0, 6.0, ((0, 32), (1, 8))),
        "sibling_value_matrix": noise(splits[4], (SIBLING_COUNT, SIBLING_SLOTS, KV_HEAD_COUNT * HEAD_SIZE), 1.0, 6.0, ((0, 32), (1, 8))),
        "prefix_keys": draw_prefix_keys(jax.random.fold_in(splits[8], 71), 0),
        "prefix_value_matrix": noise(splits[6], (PREFIX_TOKENS, KV_HEAD_COUNT * HEAD_SIZE), 1.0, 6.0, ((0, 256),)),
        "lengths": uneven(splits[7], SIBLING_COUNT, SIBLING_COUNT * SIBLING_SLOTS * 5 // 8, SIBLING_SLOTS, 2).astype(jnp.int32),
    }


def head_grads(query_head, grad_head, delta_head, prefix_key, prefix_value, sibling_key, sibling_value, causal, score_scale):
    prefix_scores = jnp.dot(query_head, prefix_key.T, preferred_element_type=jnp.float32) * score_scale
    sibling_scores = jnp.dot(query_head, sibling_key.T, preferred_element_type=jnp.float32) * score_scale
    sibling_scores = jnp.where(causal, sibling_scores, -jnp.inf)
    row_max = jnp.maximum(lax.optimization_barrier(jnp.max(prefix_scores, 1)), lax.optimization_barrier(jnp.max(sibling_scores, 1)))
    row_sum = lax.optimization_barrier(jnp.sum(jnp.exp(prefix_scores - row_max[:, None]), 1)) + lax.optimization_barrier(jnp.sum(jnp.exp(sibling_scores - row_max[:, None]), 1))
    log_norm = row_max + jnp.log(row_sum)
    prefix_probs = jnp.exp(prefix_scores - log_norm[:, None])
    sibling_probs = jnp.exp(sibling_scores - log_norm[:, None])
    prefix_dprobs = jnp.dot(grad_head, prefix_value.T, preferred_element_type=jnp.float32)
    sibling_dprobs = jnp.dot(grad_head, sibling_value.T, preferred_element_type=jnp.float32)
    prefix_dscores = (prefix_probs * (prefix_dprobs - delta_head[:, None])).astype(jnp.bfloat16)
    sibling_dscores = (sibling_probs * (sibling_dprobs - delta_head[:, None])).astype(jnp.bfloat16)
    prefix_dv = jnp.dot(prefix_probs.astype(jnp.bfloat16).T, grad_head, preferred_element_type=jnp.float32)
    prefix_dk = jnp.dot(prefix_dscores.T, query_head, preferred_element_type=jnp.float32) * score_scale
    sibling_dv = jnp.dot(sibling_probs.astype(jnp.bfloat16).T, grad_head, preferred_element_type=jnp.float32)
    sibling_dk = jnp.dot(sibling_dscores.T, query_head, preferred_element_type=jnp.float32) * score_scale
    prefix_blocks = jnp.einsum('isct,sctd->cid', prefix_dscores.reshape(SIBLING_SLOTS, N_SIB, N_CTX, PS).astype(jnp.float32), prefix_key.reshape(N_SIB, N_CTX, PS, HEAD_SIZE).astype(jnp.float32))
    sibling_blocks = jnp.einsum('icr,crd->cid', sibling_dscores.reshape(SIBLING_SLOTS, N_CTX, R).astype(jnp.float32), sibling_key.reshape(N_CTX, R, HEAD_SIZE).astype(jnp.float32))
    block_parts = ((prefix_blocks + sibling_blocks) * score_scale).astype(jnp.bfloat16)
    block_parts = lax.optimization_barrier(block_parts).astype(jnp.float32)
    return (lax.optimization_barrier(jnp.sum(block_parts, 0)), prefix_dk, prefix_dv, sibling_dk, sibling_dv)

def reference(queries, output_gradient, forward_output, sibling_key_matrix, sibling_value_matrix, prefix_keys, prefix_value_matrix, lengths):
    score_scale = 1.0 / math.sqrt(HEAD_SIZE)
    positions = jnp.arange(SIBLING_SLOTS, dtype=jnp.int32)
    causal = positions[None, :] <= positions[:, None]

    def one_sibling(totals, sibling_data):
        query, grad_rows, saved_output, key_rows, value_rows, length = sibling_data
        live_mask = (positions < length)[None, :, None]
        live_gradient = jnp.where(live_mask, grad_rows, jnp.zeros_like(grad_rows))
        row_delta_term = lax.optimization_barrier(jnp.sum((live_gradient.astype(jnp.float32) * saved_output.astype(jnp.float32)).reshape(QUERY_PER_KV, SIBLING_SLOTS, KV_HEAD_COUNT, HEAD_SIZE), -1)).astype(jnp.bfloat16)
        row_delta_term = lax.optimization_barrier(row_delta_term).astype(jnp.float32)
        query_pieces = [[None] * KV_HEAD_COUNT for group_number in range(QUERY_PER_KV)]
        prefix_dk_heads, prefix_dv_heads, sibling_dk_heads, sibling_dv_heads = ([], [], [], [])
        for head_number in range(KV_HEAD_COUNT):
            columns = slice(head_number * HEAD_SIZE, (head_number + 1) * HEAD_SIZE)
            prefix_dk = jnp.zeros((PREFIX_TOKENS, HEAD_SIZE), jnp.float32)
            prefix_dv = jnp.zeros((PREFIX_TOKENS, HEAD_SIZE), jnp.float32)
            sibling_dk = jnp.zeros((SIBLING_SLOTS, HEAD_SIZE), jnp.float32)
            sibling_dv = jnp.zeros((SIBLING_SLOTS, HEAD_SIZE), jnp.float32)
            for group_number in range(QUERY_PER_KV):
                results = head_grads(query[group_number][:, columns], live_gradient[group_number][:, columns], row_delta_term[group_number][:, head_number], prefix_keys[:, columns], prefix_value_matrix[:, columns], key_rows[:, columns], value_rows[:, columns], causal, score_scale)
                query_pieces[group_number][head_number] = results[0]
                prefix_dk = prefix_dk + results[1]
                prefix_dv = prefix_dv + results[2]
                sibling_dk = sibling_dk + results[3]
                sibling_dv = sibling_dv + results[4]
            prefix_dk_heads.append(prefix_dk)
            prefix_dv_heads.append(prefix_dv)
            sibling_dk_heads.append(sibling_dk)
            sibling_dv_heads.append(sibling_dv)
        query_grad = jnp.stack([jnp.concatenate(query_pieces[group_number], 1) for group_number in range(QUERY_PER_KV)], 0).astype(jnp.bfloat16)
        new_totals = (totals[0] + jnp.concatenate(prefix_dk_heads, 1), totals[1] + jnp.concatenate(prefix_dv_heads, 1))
        outputs = (query_grad, jnp.concatenate(sibling_dk_heads, 1).astype(jnp.bfloat16), jnp.concatenate(sibling_dv_heads, 1).astype(jnp.bfloat16))
        return (new_totals, outputs)
    initial_values = (jnp.zeros((PREFIX_TOKENS, KV_HEAD_COUNT * HEAD_SIZE), jnp.float32), jnp.zeros((PREFIX_TOKENS, KV_HEAD_COUNT * HEAD_SIZE), jnp.float32))
    totals, outputs = lax.scan(one_sibling, initial_values, (queries, output_gradient, forward_output, sibling_key_matrix, sibling_value_matrix, lengths))
    return (outputs[0], outputs[1], outputs[2], totals[0].astype(jnp.bfloat16), totals[1].astype(jnp.bfloat16))
```

```python
import functools
import math

import jax
import jax.numpy as jnp
from jax import lax
from jax.experimental import pallas as pl
from jax.experimental.pallas import tpu as pltpu
from jax.sharding import Mesh, PartitionSpec as P

HEADS = 4
LANES = 128
ROWS = 128
GROUPS = 2
LOG2E = math.log2(math.e)
NEG = -1e30
Z = ("cb", "cq", "tp")


def dot_nt(a, b):
    return lax.dot_general(a, b, (((1,), (1,)), ((), ())), preferred_element_type=jnp.float32)


def dot_nn(a, b):
    return lax.dot_general(a, b, (((1,), (0,)), ((), ())), preferred_element_type=jnp.float32)


def vmem(n):
    return [pl.BlockSpec(memory_space=pltpu.VMEM)] * n


def cost(flops, moved, exps=0):
    return pl.CostEstimate(flops=flops, bytes_accessed=moved, transcendentals=exps)


def pack_kernel(lengths, q, g, o, k, v, pk, pv, kvm, qg):
    ctx = lax.axis_index("cb") * HEADS + lax.axis_index("cq")
    length = lengths[lax.axis_index("sib")]
    row = lax.broadcasted_iota(jnp.int32, (ROWS, LANES), 0) + ctx * ROWS
    live = row < length
    ones = jnp.ones((8, LANES), jnp.bfloat16)
    for h in range(HEADS):
        cols = slice(h * LANES, (h + 1) * LANES)
        kvm[h, 0:ROWS, :] = k[:, cols]
        kvm[h, ROWS : 2 * ROWS, :] = v[:, cols]
        deltas = []
        for slot in range(GROUPS):
            rows = slice(slot * ROWS, (slot + 1) * ROWS)
            qg[h, rows, :] = q[slot, :, cols]
            grad = jnp.where(live, g[slot, :, cols].astype(jnp.float32), 0.0)
            qg[h, GROUPS * ROWS + slot * ROWS : GROUPS * ROWS + (slot + 1) * ROWS, :] = grad.astype(
                jnp.bfloat16
            )
            prod = grad * o[slot, :, cols].astype(jnp.float32)
            high = prod.astype(jnp.bfloat16)
            low = (prod - high.astype(jnp.float32)).astype(jnp.bfloat16)
            deltas.append((dot_nt(ones, high) + dot_nt(ones, low))[0:1])
        misc = jnp.concatenate(
            [pk[:, cols].astype(jnp.float32), pv[:, cols].astype(jnp.float32)]
            + deltas
            + [jnp.zeros((6, LANES), jnp.float32)],
            axis=0,
        )
        kvm[h, 2 * ROWS : 2 * ROWS + 16, :] = misc.astype(jnp.bfloat16)


def main_kernel(
    chunk, n_sib, qg, kvm, oth_lo, oth_hi, pref,
    dq, pgrad, keep, send8, plus, minus,
    keys, values, keys_t, scores, dk_acc, dv_acc,
):
    scale = 1.0 / math.sqrt(LANES)
    cb = lax.axis_index("cb")
    tp = lax.axis_index("tp")
    half = HEADS * ROWS
    pre = n_sib * 16
    total = 2 * pre + 2 * half
    for part, base in ((0, 0), (1, pre)):
        keys[base : base + pre, :] = pref[:, part * 32 : part * 32 + 16, :].reshape(pre, LANES)
        values[base : base + pre, :] = pref[:, part * 32 + 16 : part * 32 + 32, :].reshape(pre, LANES)
    base = 2 * pre
    for slot in range(HEADS):
        src = (oth_lo if slot < 2 else oth_hi).at[slot % 2]
        keys[base + slot * ROWS : base + (slot + 1) * ROWS, :] = src[0:ROWS, :]
        values[base + slot * ROWS : base + (slot + 1) * ROWS, :] = src[ROWS : 2 * ROWS, :]
    base = 2 * pre + half
    for slot in range(HEADS):
        keys[base + slot * ROWS : base + (slot + 1) * ROWS, :] = kvm[slot, 0:ROWS, :]
        values[base + slot * ROWS : base + (slot + 1) * ROWS, :] = kvm[slot, ROWS : 2 * ROWS, :]
    for at in range(0, total, chunk):
        keys_t[:, at : at + chunk] = keys[at : at + chunk, :].astype(jnp.float32).T.astype(jnp.bfloat16)
    dk_acc[...] = jnp.zeros_like(dk_acc)
    dv_acc[...] = jnp.zeros_like(dv_acc)
    wide = GROUPS * ROWS

    @pl.loop(0, HEADS)
    def _(tile):
        queries = qg[tile, 0:wide, :]
        grads = qg[tile, wide : 2 * wide, :]
        misc = kvm[tile, 2 * ROWS : 2 * ROWS + 16, :].astype(jnp.float32)
        delta = jnp.concatenate([misc[8 + s : 9 + s] for s in range(GROUPS)], axis=1)
        position = tile * ROWS + lax.rem(lax.broadcasted_iota(jnp.int32, (chunk, wide), 1), ROWS)
        key_at = lax.broadcasted_iota(jnp.int32, (chunk, wide), 0)
        top = jnp.full((1, wide), NEG, jnp.float32)
        for at in range(0, total, chunk):
            s = dot_nt(keys[at : at + chunk, :], queries) * (scale * LOG2E)
            if at >= 2 * pre + half:
                s = jnp.where(key_at + (at - 2 * pre - half) <= position, s, NEG)
            elif at >= 2 * pre:
                s = jnp.where(cb == 1, s, NEG)
            scores[at : at + chunk, :] = s
            top = jnp.maximum(top, jnp.max(s, axis=0, keepdims=True))
        norm = jnp.zeros((1, wide), jnp.float32)
        for at in range(0, total, chunk):
            e = jnp.exp2(scores[at : at + chunk, :] - top)
            scores[at : at + chunk, :] = e
            norm = norm + jnp.sum(e, axis=0, keepdims=True)
        inverse = 1.0 / norm
        dq_t = jnp.zeros((LANES, wide), jnp.float32)
        for at in range(0, total, chunk):
            p = scores[at : at + chunk, :] * inverse
            dp = dot_nt(values[at : at + chunk, :], grads)
            ds = (p * (dp - delta)).astype(jnp.bfloat16)
            dv_acc[at : at + chunk, :] += dot_nn(p.astype(jnp.bfloat16), grads)
            dk_acc[at : at + chunk, :] += dot_nn(ds, queries)
            dq_t = dq_t + dot_nn(keys_t[:, at : at + chunk], ds)
        dq[tile, :, :] = (dq_t.T * scale).astype(jnp.bfloat16)

    for part, base in ((0, 0), (1, pre)):
        pgrad[:, part * 32 : part * 32 + 16, :] = (
            (dk_acc[base : base + pre, :] * scale).astype(jnp.bfloat16).reshape(n_sib, 16, LANES)
        )
        pgrad[:, part * 32 + 16 : part * 32 + 32, :] = (
            dv_acc[base : base + pre, :].astype(jnp.bfloat16).reshape(n_sib, 16, LANES)
        )
    for out, base, which in (
        (minus, 2 * pre, tp),
        (plus, 2 * pre, 1 - tp),
        (keep, 2 * pre + half, tp),
        (send8, 2 * pre + half, 1 - tp),
    ):
        for slot in range(HEADS):
            rows = pl.ds(pl.multiple_of(base + slot * ROWS + which * (ROWS // 2), ROWS // 2), ROWS // 2)
            out[slot, 0 : ROWS // 2, :] = (dk_acc[rows, :] * scale).astype(jnp.bfloat16)
            out[slot, ROWS // 2 : ROWS, :] = dv_acc[rows, :].astype(jnp.bfloat16)


def unpack_kernel(dq, sib, dq_out, sk_out, sv_out):
    for h in range(HEADS):
        cols = slice(h * LANES, (h + 1) * LANES)
        for slot in range(GROUPS):
            dq_out[slot, :, cols] = dq[h, slot * ROWS : (slot + 1) * ROWS, :]
        sk_out[:, cols] = sib[h, 0 : ROWS // 2, :]
        sv_out[:, cols] = sib[h, ROWS // 2 : ROWS, :]


def ring_index(position):
    return (position % 8) * 2 + position // 8


def ring(shift, sources=range(16)):
    return [(ring_index(p), ring_index((p + shift) % 16)) for p in sources]


def on_device(n_sib, queries, gradient, forward, sib_k, sib_v, pre_k, pre_v, lengths):
    bf16 = jnp.bfloat16
    shape = jax.ShapeDtypeStruct
    cb, tp = lax.axis_index("cb"), lax.axis_index("tp")
    late = [p for p in range(16) if p % 8 >= 4]

    kvm, qg = pl.pallas_call(
        pack_kernel,
        out_shape=(shape((HEADS, 272, LANES), bf16), shape((HEADS, 512, LANES), bf16)),
        in_specs=[pl.BlockSpec(memory_space=pltpu.SMEM)] + vmem(7),
        out_specs=tuple(vmem(2)),
        cost_estimate=cost(1 << 20, 2 << 20),
        name="pack_heads",
    )(lengths, queries[0], gradient[0], forward[0], sib_k[0], sib_v[0], pre_k, pre_v)

    kvm = lax.all_to_all(kvm, "cq", 0, 0)
    qg = lax.all_to_all(qg, "cq", 0, 0)
    own_rows = jnp.concatenate(
        [kvm[:, 256:260].reshape(16, LANES), kvm[:, 260:264].reshape(16, LANES)], 0
    )
    other_rows = lax.ppermute(own_rows, "cb", [(0, 1), (1, 0)])
    own_kv = kvm[:, 0:256]
    oth_lo = lax.ppermute(own_kv[0:2], Z, ring(4, [p for p in range(16) if p % 8 < 4]))
    oth_hi = lax.ppermute(own_kv[2:4], Z, ring(-4, [p for p in range(16) if p % 8 < 4]))
    spread = jnp.broadcast_to(jnp.concatenate([own_rows, other_rows], 0)[None], (n_sib, 64, LANES))
    pref = lax.all_to_all(spread, "sib", 0, 0)

    total = 2 * n_sib * 16 + 2 * HEADS * ROWS
    wide = GROUPS * ROWS
    piece = shape((HEADS, ROWS, LANES), bf16)
    dq, pgrad, keep, send8, plus, minus = pl.pallas_call(
        functools.partial(main_kernel, min(256, n_sib * 16), n_sib),
        out_shape=(
            shape((HEADS, wide, LANES), bf16),
            shape((n_sib, 64, LANES), bf16),
            piece,
            piece,
            piece,
            piece,
        ),
        in_specs=vmem(5),
        out_specs=tuple(vmem(6)),
        scratch_shapes=[
            pltpu.VMEM((total, LANES), bf16),
            pltpu.VMEM((total, LANES), bf16),
            pltpu.VMEM((LANES, total), bf16),
            pltpu.VMEM((total, wide), jnp.float32),
            pltpu.VMEM((total, LANES), jnp.float32),
            pltpu.VMEM((total, LANES), jnp.float32),
        ],
        compiler_params=pltpu.CompilerParams(vmem_limit_bytes=32 << 20),
        cost_estimate=cost(10 * HEADS * wide * total * LANES, 4 << 20, HEADS * wide * total),
        name="attention_grads",
    )(qg, kvm, oth_lo, oth_hi, pref)

    got8 = lax.ppermute(send8, Z, ring(8))
    got_plus = lax.ppermute(plus, Z, ring(4, late))
    got_minus = lax.ppermute(minus, Z, ring(-4, late))

    pparts = lax.all_to_all(pgrad, "sib", 0, 0)
    psum = jnp.sum(pparts.astype(jnp.float32), 0).reshape(2, 2, HEADS, 2, 2, LANES)
    plus_tp = jnp.where(cb == 1, 1 - tp, tp)

    def rows_for(part, which):
        return lax.dynamic_index_in_dim(psum[part], which, 2, False).reshape(16, LANES)

    mine = (
        rows_for(0, tp)
        + lax.ppermute(rows_for(0, 1 - tp), Z, ring(8))
        + lax.ppermute(rows_for(1, plus_tp), Z, ring(4))
        + lax.ppermute(rows_for(1, 1 - plus_tp), Z, ring(-4))
    )

    f32 = jnp.float32
    sib = (
        keep.astype(f32) + got8.astype(f32) + got_plus.astype(f32) + got_minus.astype(f32)
    ).astype(bf16)
    back = lax.all_to_all(jnp.concatenate([dq, sib], 1), "cq", 0, 0)
    small = lax.all_to_all(mine.reshape(2, HEADS, 2, LANES).swapaxes(0, 1), "cq", 0, 0)
    out_k = small[:, 0].swapaxes(0, 1).reshape(2, HEADS * LANES).astype(bf16)
    out_v = small[:, 1].swapaxes(0, 1).reshape(2, HEADS * LANES).astype(bf16)

    dq_out, sk_out, sv_out = pl.pallas_call(
        unpack_kernel,
        out_shape=(
            shape((GROUPS, ROWS, HEADS * LANES), bf16),
            shape((ROWS // 2, HEADS * LANES), bf16),
            shape((ROWS // 2, HEADS * LANES), bf16),
        ),
        in_specs=vmem(2),
        out_specs=tuple(vmem(3)),
        cost_estimate=cost(1 << 10, 1 << 20),
        name="unpack_heads",
    )(back[:, 0:wide], back[:, wide:])
    return dq_out[None], sk_out[None], sv_out[None], out_k, out_v


def solution(mesh):
    n_sib, n_ctx, n_tp = mesh.shape["sib"], mesh.shape["ctx"], mesh.shape["tp"]
    fine = Mesh(
        mesh.devices.reshape(n_sib, n_ctx // HEADS, HEADS, n_tp), ("sib", "cb", "cq", "tp")
    )
    ctx = ("cb", "cq")
    heads = P("sib", "tp", ctx, None)
    return jax.shard_map(
        functools.partial(on_device, n_sib),
        mesh=fine,
        in_specs=(
            heads,
            heads,
            heads,
            P("sib", ctx, None),
            P("sib", ctx, None),
            P(("sib",) + ctx, None),
            P(("sib",) + ctx, None),
            P(),
        ),
        out_specs=(
            heads,
            P("sib", ctx + ("tp",), None),
            P("sib", ctx + ("tp",), None),
            P(("sib",) + ctx + ("tp",), None),
            P(("sib",) + ctx + ("tp",), None),
        ),
        check_vma=False,
    )
```

```python
import functools
import math

import jax
import jax.numpy as jnp
from jax import lax
from jax.experimental import pallas as pl
from jax.experimental.pallas import tpu as pltpu
from jax.sharding import Mesh, PartitionSpec as P

HEADS = 4
LANES = 128
ROWS = 128
GROUPS = 2
LOG2E = math.log2(math.e)
NEG = -1e30
Z = ("cb", "cq", "tp")


def dot_nt(a, b):
    return lax.dot_general(a, b, (((1,), (1,)), ((), ())), preferred_element_type=jnp.float32)


def dot_nn(a, b):
    return lax.dot_general(a, b, (((1,), (0,)), ((), ())), preferred_element_type=jnp.float32)


def vmem(n):
    return [pl.BlockSpec(memory_space=pltpu.VMEM)] * n


def cost(flops, moved, exps=0):
    return pl.CostEstimate(flops=flops, bytes_accessed=moved, transcendentals=exps)


def pack_kernel(lengths, q, g, o, k, v, bulk):
    ctx = lax.axis_index("cb") * HEADS + lax.axis_index("cq")
    length = lengths[lax.axis_index("sib")]
    row = lax.broadcasted_iota(jnp.int32, (ROWS, LANES), 0) + ctx * ROWS
    live = row < length
    ones = jnp.ones((8, LANES), jnp.bfloat16)
    for h in range(HEADS):
        cols = slice(h * LANES, (h + 1) * LANES)
        bulk[h, 4 * ROWS : 5 * ROWS, :] = k[:, cols]
        bulk[h, 5 * ROWS : 6 * ROWS, :] = v[:, cols]
        deltas = []
        for slot in range(GROUPS):
            rows = slice(slot * ROWS, (slot + 1) * ROWS)
            bulk[h, rows, :] = q[slot, :, cols]
            grad = jnp.where(live, g[slot, :, cols].astype(jnp.float32), 0.0)
            bulk[h, GROUPS * ROWS + slot * ROWS : GROUPS * ROWS + (slot + 1) * ROWS, :] = grad.astype(
                jnp.bfloat16
            )
            prod = grad * o[slot, :, cols].astype(jnp.float32)
            high = prod.astype(jnp.bfloat16)
            low = (prod - high.astype(jnp.float32)).astype(jnp.bfloat16)
            deltas.append((dot_nt(ones, high) + dot_nt(ones, low))[0:1])
        rest = jnp.concatenate(deltas + [jnp.zeros((14, LANES), jnp.float32)], axis=0)
        bulk[h, 6 * ROWS : 6 * ROWS + 16, :] = rest.astype(jnp.bfloat16)


def pack_prefix_kernel(pk, pv, pre):
    for h in range(HEADS):
        cols = slice(h * LANES, (h + 1) * LANES)
        own = jnp.concatenate(
            [
                pk[:, cols].astype(jnp.float32),
                pv[:, cols].astype(jnp.float32),
                jnp.zeros((8, LANES), jnp.float32),
            ],
            axis=0,
        ).astype(jnp.bfloat16)
        for half in range(2):
            pre[half * HEADS + h] = own


def spread_kernel(pre, out):
    rows = [pre[at].astype(jnp.float32) for at in range(2 * HEADS)]
    block = []
    for half in range(2):
        mine = rows[half * HEADS : (half + 1) * HEADS]
        block += [r[0:4] for r in mine] + [r[4:8] for r in mine]
    block = jnp.concatenate(block, axis=0).astype(jnp.bfloat16)
    for at in range(out.shape[0]):
        out[at] = block


def load_keys(pref, keys, values):
    pre = pref.shape[0] * 16
    for part in range(2):
        rows = slice(part * pre, (part + 1) * pre)
        keys[rows, :] = pref[:, part * 32 : part * 32 + 16, :].reshape(pre, LANES)
        values[rows, :] = pref[:, part * 32 + 16 : part * 32 + 32, :].reshape(pre, LANES)


def tile_data(bulk, step):
    wide = GROUPS * ROWS
    rest = bulk[step, 6 * ROWS : 6 * ROWS + 16, :].astype(jnp.float32)
    delta = jnp.concatenate([rest[s : s + 1] for s in range(GROUPS)], axis=1)
    return bulk[step, 0:wide, :], bulk[step, wide : 2 * wide, :], delta


def gather_bulk(bulk, own, far1, far2, far3):
    bulk[0] = own[lax.axis_index("cq")]
    for step, received in ((1, far1), (2, far2), (3, far3)):
        bulk[step] = received[...]


def transpose_keys(keys, keys_t, start, stop, chunk):
    for at in range(start, stop, chunk):
        keys_t[:, at - start : at - start + chunk] = (
            keys[at : at + chunk, :].astype(jnp.float32).T.astype(jnp.bfloat16)
        )


def load_sibling(bulk, oth_lo, oth_hi, keys, values, base):
    cq = lax.axis_index("cq")
    half = HEADS * ROWS
    for step in range(HEADS):
        at = jnp.bitwise_xor(cq, step) * ROWS
        src = (oth_lo if step < 2 else oth_hi).at[step % 2]
        rows = pl.ds(pl.multiple_of(base + at, ROWS), ROWS)
        keys[rows, :] = src[0:ROWS, :]
        if values is not None:
            values[rows, :] = src[ROWS : 2 * ROWS, :]
        rows = pl.ds(pl.multiple_of(base + half + at, ROWS), ROWS)
        keys[rows, :] = bulk[step, 4 * ROWS : 5 * ROWS, :]
        if values is not None:
            values[rows, :] = bulk[step, 5 * ROWS : 6 * ROWS, :]


def sibling_scores(keys, queries, at, base, tile):
    half = HEADS * ROWS
    chunk = keys.shape[0]
    s = dot_nt(keys, queries) * (LOG2E / math.sqrt(LANES))
    if at >= base + half:
        position = tile * ROWS + lax.rem(lax.broadcasted_iota(jnp.int32, s.shape, 1), ROWS)
        key_at = lax.broadcasted_iota(jnp.int32, s.shape, 0) + (at - base - half)
        return jnp.where(key_at <= position, s, NEG)
    if at >= base:
        return jnp.where(lax.axis_index("cb") == 1, s, NEG)
    return s


def prefix_kernel(
    chunk, own, far1, far2, far3, oth_lo, oth_hi, pref,
    pgrad, norms, dq_part,
    keys, values, keys_t, scores, dk_acc, dv_acc, bulk,
):
    scale = 1.0 / math.sqrt(LANES)
    n_sib = pref.shape[0]
    pre = n_sib * 32
    total = keys.shape[0]
    wide = GROUPS * ROWS
    gather_bulk(bulk, own, far1, far2, far3)
    load_keys(pref, keys, values)
    load_sibling(bulk, oth_lo, oth_hi, keys, None, pre)
    transpose_keys(keys, keys_t, 0, pre, chunk)
    dk_acc[...] = jnp.zeros_like(dk_acc)
    dv_acc[...] = jnp.zeros_like(dv_acc)

    @pl.loop(0, HEADS)
    def _(step):
        tile = jnp.bitwise_xor(lax.axis_index("cq"), step)
        queries, grads, delta = tile_data(bulk, step)
        top = jnp.full((1, wide), NEG, jnp.float32)
        for at in range(0, total, chunk):
            s = sibling_scores(keys[at : at + chunk, :], queries, at, pre, tile)
            scores[at : at + chunk, :] = s
            top = jnp.maximum(top, jnp.max(s, axis=0, keepdims=True))
        norm = jnp.zeros((1, wide), jnp.float32)
        for at in range(0, total, chunk):
            e = jnp.exp2(scores[at : at + chunk, :] - top)
            if at < pre:
                scores[at : at + chunk, :] = e
            norm = norm + jnp.sum(e, axis=0, keepdims=True)
        norms[step] = jnp.broadcast_to(top + jnp.log2(norm), (8, wide))
        inverse = 1.0 / norm
        dq_t = jnp.zeros((LANES, wide), jnp.float32)
        for at in range(0, pre, chunk):
            rows = slice(at, at + chunk)
            p = scores[rows, :] * inverse
            dp = dot_nt(values[rows, :], grads)
            ds = (p * (dp - delta)).astype(jnp.bfloat16)
            dv_acc[rows, :] += dot_nn(p.astype(jnp.bfloat16), grads)
            dk_acc[rows, :] += dot_nn(ds, queries)
            dq_t = dq_t + dot_nn(keys_t[:, rows], ds)
        dq_part[step, :, :] = dq_t

    for part in range(2):
        rows = slice(part * pre // 2, (part + 1) * pre // 2)
        pgrad[:, part * 32 : part * 32 + 16, :] = (
            (dk_acc[rows, :] * scale).astype(jnp.bfloat16).reshape(n_sib, 16, LANES)
        )
        pgrad[:, part * 32 + 16 : part * 32 + 32, :] = (
            dv_acc[rows, :].astype(jnp.bfloat16).reshape(n_sib, 16, LANES)
        )


def sibling_kernel(
    chunk, own, far1, far2, far3, oth_lo, oth_hi, norms, dq_part,
    dq0, dq1, dq2, dq3, sgrad,
    keys, values, keys_t, dk_acc, dv_acc, bulk, dq,
):
    scale = 1.0 / math.sqrt(LANES)
    cb = lax.axis_index("cb")
    total = keys.shape[0]
    gather_bulk(bulk, own, far1, far2, far3)
    load_sibling(bulk, oth_lo, oth_hi, keys, values, 0)
    transpose_keys(keys, keys_t, 0, total, chunk)
    dk_acc[...] = jnp.zeros_like(dk_acc)
    dv_acc[...] = jnp.zeros_like(dv_acc)

    @pl.loop(0, HEADS)
    def _(step):
        tile = jnp.bitwise_xor(lax.axis_index("cq"), step)
        queries, grads, delta = tile_data(bulk, step)
        norm = norms[step][0:1]
        dq_t = dq_part[step]
        for at in range(0, total, chunk):
            rows = slice(at, at + chunk)
            p = jnp.exp2(sibling_scores(keys[rows, :], queries, at, 0, tile) - norm)
            dp = dot_nt(values[rows, :], grads)
            ds = (p * (dp - delta)).astype(jnp.bfloat16)
            dv_acc[rows, :] += dot_nn(p.astype(jnp.bfloat16), grads)
            dk_acc[rows, :] += dot_nn(ds, queries)
            dq_t = dq_t + dot_nn(keys_t[:, rows], ds)
        dq[step, :, :] = (dq_t.T * scale).astype(jnp.bfloat16)

    for step, out in enumerate((dq0, dq1, dq2, dq3)):
        out[...] = dq[step]
    for base, owner in ((0, 1 - cb), (HEADS * ROWS, cb)):
        for piece in range(2 * HEADS):
            rows = slice(base + piece * (ROWS // 2), base + (piece + 1) * (ROWS // 2))
            at = owner * 2 * HEADS + piece
            sgrad[at, 0 : ROWS // 2, :] = (dk_acc[rows, :] * scale).astype(jnp.bfloat16)
            sgrad[at, ROWS // 2 : ROWS, :] = dv_acc[rows, :].astype(jnp.bfloat16)


def prefix_sum_kernel(parts, sgrad, out):
    total = jnp.sum(parts[...].astype(jnp.float32), axis=0)
    for part in range(2):
        for piece in range(2 * HEADS):
            at = part * 32 + piece * 2
            rows = jnp.concatenate(
                [total[at : at + 2], total[at + 16 : at + 18], jnp.zeros((12, LANES), jnp.float32)],
                axis=0,
            )
            out[part * 2 * HEADS + piece, :, :] = rows.astype(jnp.bfloat16)


def unpack_kernel(dq0, dq1, dq2, dq3, parts, dq_out, sk_out, sv_out, pk_out, pv_out):
    cq = lax.axis_index("cq")
    half = ROWS // 2
    for step, dq in enumerate((dq0, dq1, dq2, dq3)):
        head = jnp.bitwise_xor(cq, step)
        cols = pl.ds(pl.multiple_of(head * LANES, LANES), LANES)
        for slot in range(GROUPS):
            dq_out[slot, :, cols] = dq[slot * ROWS : (slot + 1) * ROWS, :]
    for head in range(HEADS):
        cols = slice(head * LANES, (head + 1) * LANES)
        total = sum(
            parts[(b * HEADS + head) * 2 + t].astype(jnp.float32) for b in range(2) for t in range(2)
        ).astype(jnp.bfloat16)
        sk_out[:, cols] = total[0:half]
        sv_out[:, cols] = total[half:ROWS]
        pk_out[:, cols] = total[ROWS : ROWS + 2]
        pv_out[:, cols] = total[ROWS + 2 : ROWS + 4]


def ring_index(position):
    return (position % 8) * 2 + position // 8


def ring(shift, sources=range(16)):
    return [(ring_index(p), ring_index((p + shift) % 16)) for p in sources]


def on_device(n_sib, queries, gradient, forward, sib_k, sib_v, pre_k, pre_v, lengths):
    bf16 = jnp.bfloat16
    shape = jax.ShapeDtypeStruct

    pre = pl.pallas_call(
        pack_prefix_kernel,
        out_shape=shape((2 * HEADS, 16, LANES), bf16),
        in_specs=vmem(2),
        out_specs=vmem(1)[0],
        cost_estimate=cost(1 << 10, 1 << 16),
        name="pack_prefix",
    )(pre_k, pre_v)
    bulk = pl.pallas_call(
        pack_kernel,
        out_shape=shape((HEADS, 784, LANES), bf16),
        in_specs=[pl.BlockSpec(memory_space=pltpu.SMEM)] + vmem(5),
        out_specs=vmem(1)[0],
        cost_estimate=cost(1 << 20, 2 << 20),
        name="pack_heads",
    )(lengths, queries[0], gradient[0], forward[0], sib_k[0], sib_v[0])
    cq = lax.axis_index("cq")

    def swap(array, step):
        return lax.ppermute(array, "cq", [(i, i ^ step) for i in range(HEADS)])

    def slot(array, step):
        return lax.dynamic_index_in_dim(array, jnp.bitwise_xor(cq, step), 0, False)

    far = [swap(slot(bulk, d), d) for d in (1, 2, 3)]
    pre = lax.all_to_all(pre, ("cb", "cq"), 0, 0)
    early = [p for p in range(16) if p % 8 < 4]
    pairs = [a[4 * ROWS : 6 * ROWS] for a in [slot(bulk, 0)] + far]
    oth_lo = lax.ppermute(jnp.stack(pairs[0:2]), Z, ring(4, early))
    oth_hi = lax.ppermute(jnp.stack(pairs[2:4]), Z, ring(-4, early))
    spread = pl.pallas_call(
        spread_kernel,
        out_shape=shape((n_sib, 64, LANES), bf16),
        in_specs=vmem(1),
        out_specs=vmem(1)[0],
        cost_estimate=cost(1 << 18, 1 << 19),
        name="spread_prefix",
    )(pre)
    pref = lax.all_to_all(spread, "sib", 0, 0)

    chunk = min(256, n_sib * 16)
    pre_rows, sib_rows = 32 * n_sib, 2 * HEADS * ROWS
    wide = GROUPS * ROWS
    pgrad, norms, dq_part = pl.pallas_call(
        functools.partial(prefix_kernel, chunk),
        out_shape=(
            shape((n_sib, 64, LANES), bf16),
            shape((HEADS, 8, wide), jnp.float32),
            shape((HEADS, LANES, wide), jnp.float32),
        ),
        in_specs=vmem(7),
        out_specs=tuple(vmem(3)),
        scratch_shapes=[
            pltpu.VMEM((pre_rows + sib_rows, LANES), bf16),
            pltpu.VMEM((pre_rows, LANES), bf16),
            pltpu.VMEM((LANES, pre_rows), bf16),
            pltpu.VMEM((pre_rows + sib_rows, wide), jnp.float32),
            pltpu.VMEM((pre_rows, LANES), jnp.float32),
            pltpu.VMEM((pre_rows, LANES), jnp.float32),
            pltpu.VMEM((HEADS, 784, LANES), bf16),
        ],
        compiler_params=pltpu.CompilerParams(vmem_limit_bytes=32 << 20),
        cost_estimate=cost(6 * HEADS * wide * 2048 * LANES, 4 << 20, HEADS * wide * 2048),
        name="prefix_grads",
    )(bulk, *far, oth_lo, oth_hi, pref)
    *dq, sgrad = pl.pallas_call(
        functools.partial(sibling_kernel, chunk),
        out_shape=(shape((wide, LANES), bf16),) * 4 + (shape((16, ROWS + 16, LANES), bf16),),
        in_specs=vmem(8),
        out_specs=tuple(vmem(5)),
        scratch_shapes=[
            pltpu.VMEM((sib_rows, LANES), bf16),
            pltpu.VMEM((sib_rows, LANES), bf16),
            pltpu.VMEM((LANES, sib_rows), bf16),
            pltpu.VMEM((sib_rows, LANES), jnp.float32),
            pltpu.VMEM((sib_rows, LANES), jnp.float32),
            pltpu.VMEM((HEADS, 784, LANES), bf16),
            pltpu.VMEM((HEADS, wide, LANES), bf16),
        ],
        compiler_params=pltpu.CompilerParams(vmem_limit_bytes=32 << 20),
        cost_estimate=cost(10 * HEADS * wide * 1024 * LANES, 4 << 20, HEADS * wide * 1024),
        name="sibling_grads",
    )(bulk, *far, oth_lo, oth_hi, norms, dq_part)
    dq = [dq[0]] + [swap(dq[d], d) for d in (1, 2, 3)]

    parts = lax.all_to_all(pgrad, "sib", 0, 0)
    owners = pl.pallas_call(
        prefix_sum_kernel,
        out_shape=shape((16, ROWS + 16, LANES), bf16),
        grid=(1,),
        in_specs=[
            pl.BlockSpec((n_sib, 64, LANES), lambda i: (0, 0, 0)),
            pl.BlockSpec(memory_space=pl.ANY),
        ],
        out_specs=pl.BlockSpec((16, 16, LANES), lambda i: (0, ROWS // 16, 0)),
        input_output_aliases={1: 0},
        cost_estimate=cost(1 << 18, 1 << 19),
        name="prefix_sums",
    )(parts, sgrad)
    owners = lax.all_to_all(owners, Z, 0, 0)

    dq_out, sk_out, sv_out, pk_out, pv_out = pl.pallas_call(
        unpack_kernel,
        out_shape=(
            shape((GROUPS, ROWS, HEADS * LANES), bf16),
            shape((ROWS // 2, HEADS * LANES), bf16),
            shape((ROWS // 2, HEADS * LANES), bf16),
            shape((2, HEADS * LANES), bf16),
            shape((2, HEADS * LANES), bf16),
        ),
        in_specs=vmem(5),
        out_specs=tuple(vmem(5)),
        cost_estimate=cost(1 << 18, 1 << 20),
        name="unpack_heads",
    )(*dq, owners)
    return dq_out[None], sk_out[None], sv_out[None], pk_out, pv_out


def solution(mesh):
    n_sib, n_ctx, n_tp = mesh.shape["sib"], mesh.shape["ctx"], mesh.shape["tp"]
    fine = Mesh(
        mesh.devices.reshape(n_sib, n_ctx // HEADS, HEADS, n_tp), ("sib", "cb", "cq", "tp")
    )
    ctx = ("cb", "cq")
    heads = P("sib", "tp", ctx, None)
    return jax.shard_map(
        functools.partial(on_device, n_sib),
        mesh=fine,
        in_specs=(
            heads,
            heads,
            heads,
            P("sib", ctx, None),
            P("sib", ctx, None),
            P(("sib",) + ctx, None),
            P(("sib",) + ctx, None),
            P(),
        ),
        out_specs=(
            heads,
            P("sib", ctx + ("tp",), None),
            P("sib", ctx + ("tp",), None),
            P(("sib",) + ctx + ("tp",), None),
            P(("sib",) + ctx + ("tp",), None),
        ),
        check_vma=False,
    )
```

```python
import functools
import math

import jax
import jax.numpy as jnp
from jax import lax
from jax.experimental import pallas as pl
from jax.experimental.pallas import tpu as pltpu
from jax.sharding import Mesh, PartitionSpec as P

HEADS = 4
LANES = 128
ROWS = 128
GROUPS = 2
LOG2E = math.log2(math.e)
NEG = -1e30
Z = ("cb", "cq", "tp")
NORMS_COST = 1 << 33
PACK_COST = 1 << 33
GRADS_COST = 1 << 36
MERGE_COST = 1 << 36
SPREAD_COST = 1 << 18


def dot_nt(a, b):
    return lax.dot_general(a, b, (((1,), (1,)), ((), ())), preferred_element_type=jnp.float32)


def dot_nn(a, b):
    return lax.dot_general(a, b, (((1,), (0,)), ((), ())), preferred_element_type=jnp.float32)


def vmem(n):
    return [pl.BlockSpec(memory_space=pltpu.VMEM)] * n


def cost(flops, moved, exps=0):
    return pl.CostEstimate(flops=flops, bytes_accessed=moved, transcendentals=exps)


def pack_kernel(lengths, q, g, o, k, v, pre, own, far1, far2, far3):
    cq = lax.axis_index("cq")
    ctx = lax.axis_index("cb") * HEADS + cq
    length = lengths[lax.axis_index("sib")]
    row = lax.broadcasted_iota(jnp.int32, (ROWS, LANES), 0) + ctx * ROWS
    live = row < length
    ones = jnp.ones((8, LANES), jnp.bfloat16)
    for step, out in enumerate((own, far1, far2, far3)):
        head = jnp.bitwise_xor(cq, step)
        cols = pl.ds(pl.multiple_of(head * LANES, LANES), LANES)
        out[4 * ROWS : 5 * ROWS, :] = k[:, cols]
        out[5 * ROWS : 6 * ROWS, :] = v[:, cols]
        deltas = []
        for slot in range(GROUPS):
            rows = slice(slot * ROWS, (slot + 1) * ROWS)
            out[rows, :] = q[slot, :, cols]
            grad = jnp.where(live, g[slot, :, cols].astype(jnp.float32), 0.0)
            rows = slice((GROUPS + slot) * ROWS, (GROUPS + slot + 1) * ROWS)
            out[rows, :] = grad.astype(jnp.bfloat16)
            prod = grad * o[slot, :, cols].astype(jnp.float32)
            high = prod.astype(jnp.bfloat16)
            low = (prod - high.astype(jnp.float32)).astype(jnp.bfloat16)
            deltas.append((dot_nt(ones, high) + dot_nt(ones, low))[0:1])
        rest = jnp.concatenate(deltas + [jnp.zeros((14, LANES), jnp.float32)], axis=0)
        out[6 * ROWS : 6 * ROWS + 16, :] = rest.astype(jnp.bfloat16)


def pack_prefix_kernel(pk, pv, pre):
    for head in range(HEADS):
        cols = slice(head * LANES, (head + 1) * LANES)
        rows = jnp.concatenate(
            [
                pk[:, cols].astype(jnp.float32),
                pv[:, cols].astype(jnp.float32),
                jnp.zeros((8, LANES), jnp.float32),
            ],
            axis=0,
        ).astype(jnp.bfloat16)
        for half in range(2):
            pre[half * HEADS + head] = rows


def spread_kernel(pre, out):
    rows = [pre[at].astype(jnp.float32) for at in range(2 * HEADS)]
    block = []
    for half in range(2):
        mine = rows[half * HEADS : (half + 1) * HEADS]
        block += [r[0:4] for r in mine] + [r[4:8] for r in mine]
    block = jnp.concatenate(block, axis=0).astype(jnp.bfloat16)
    for at in range(out.shape[0]):
        out[at] = block


def load_keys(pref, keys, values):
    pre = pref.shape[0] * 16
    for part in range(2):
        rows = slice(part * pre, (part + 1) * pre)
        keys[rows, :] = pref[:, part * 32 : part * 32 + 16, :].reshape(pre, LANES)
        values[rows, :] = pref[:, part * 32 + 16 : part * 32 + 32, :].reshape(pre, LANES)


def tile_data(bulk, step):
    wide = GROUPS * ROWS
    rest = bulk[step, 6 * ROWS : 6 * ROWS + 16, :].astype(jnp.float32)
    delta = jnp.concatenate([rest[s : s + 1] for s in range(GROUPS)], axis=1)
    return bulk[step, 0:wide, :], bulk[step, wide : 2 * wide, :], delta


def gather_bulk(bulk, own, far1, far2, far3):
    for step, received in enumerate((own, far1, far2, far3)):
        bulk[step] = received[...]


def transpose_keys(keys, keys_t, start, stop, chunk):
    for at in range(start, stop, chunk):
        keys_t[:, at - start : at - start + chunk] = (
            keys[at : at + chunk, :].astype(jnp.float32).T.astype(jnp.bfloat16)
        )


def load_sibling(bulk, oth_lo, oth_hi, keys, values, base):
    cq = lax.axis_index("cq")
    half = HEADS * ROWS
    for step in range(HEADS):
        at = jnp.bitwise_xor(cq, step) * ROWS
        src = (oth_lo if step < 2 else oth_hi).at[step % 2]
        rows = pl.ds(pl.multiple_of(base + at, ROWS), ROWS)
        keys[rows, :] = src[0:ROWS, :]
        if values is not None:
            values[rows, :] = src[ROWS : 2 * ROWS, :]
        rows = pl.ds(pl.multiple_of(base + half + at, ROWS), ROWS)
        keys[rows, :] = bulk[step, 4 * ROWS : 5 * ROWS, :]
        if values is not None:
            values[rows, :] = bulk[step, 5 * ROWS : 6 * ROWS, :]


def sibling_scores(keys, queries, at, tile):
    half = HEADS * ROWS
    s = dot_nt(keys, queries) * (LOG2E / math.sqrt(LANES))
    if at >= half:
        position = tile * ROWS + lax.rem(lax.broadcasted_iota(jnp.int32, s.shape, 1), ROWS)
        key_at = lax.broadcasted_iota(jnp.int32, s.shape, 0) + (at - half)
        return jnp.where(key_at <= position, s, NEG)
    return jnp.where(lax.axis_index("cb") == 1, s, NEG)


def norms_kernel(chunk, own, far1, far2, far3, pref, norms, keys, bulk):
    n_sib = pref.shape[0]
    pre = n_sib * 32
    wide = GROUPS * ROWS
    gather_bulk(bulk, own, far1, far2, far3)
    for part in range(2):
        rows = slice(part * pre // 2, (part + 1) * pre // 2)
        keys[rows, :] = pref[:, part * 32 : part * 32 + 16, :].reshape(pre // 2, LANES)

    @pl.loop(0, HEADS)
    def _(step):
        queries, grads, delta = tile_data(bulk, step)
        top = jnp.full((1, wide), NEG, jnp.float32)
        norm = jnp.zeros((1, wide), jnp.float32)
        for at in range(0, pre, chunk):
            s = dot_nt(keys[at : at + chunk, :], queries) * (LOG2E / math.sqrt(LANES))
            top, norm = online(s, top, norm)
        norms[step] = jnp.broadcast_to(top + jnp.log2(norm), (8, wide))


def online(s, top, norm):
    higher = jnp.maximum(top, jnp.max(s, axis=0, keepdims=True))
    added = jnp.sum(jnp.exp2(s - higher), axis=0, keepdims=True)
    return higher, norm * jnp.exp2(top - higher) + added


def sibling_kernel(
    chunk, own, far1, far2, far3, oth_lo, oth_hi, pre_norms,
    keep, send8, plus, minus, norms, dq_part,
    keys, values, keys_t, scores, dk_acc, dv_acc, bulk,
):
    scale = 1.0 / math.sqrt(LANES)
    total = keys.shape[0]
    half = HEADS * ROWS
    wide = GROUPS * ROWS
    gather_bulk(bulk, own, far1, far2, far3)
    load_sibling(bulk, oth_lo, oth_hi, keys, values, 0)
    transpose_keys(keys, keys_t, 0, total, chunk)
    dk_acc[...] = jnp.zeros_like(dk_acc)
    dv_acc[...] = jnp.zeros_like(dv_acc)

    @pl.loop(0, HEADS)
    def _(step):
        tile = jnp.bitwise_xor(lax.axis_index("cq"), step)
        queries, grads, delta = tile_data(bulk, step)
        top = pre_norms[step][0:1]
        norm = jnp.ones((1, wide), jnp.float32)
        tops = []
        for at in range(0, total, chunk):
            s = sibling_scores(keys[at : at + chunk, :], queries, at, tile)
            higher = jnp.maximum(top, jnp.max(s, axis=0, keepdims=True))
            e = jnp.exp2(s - higher)
            scores[at : at + chunk, :] = e
            norm = norm * jnp.exp2(top - higher) + jnp.sum(e, axis=0, keepdims=True)
            top = higher
            tops.append(top)
        log_norm = top + jnp.log2(norm)
        norms[step] = jnp.broadcast_to(log_norm, (8, wide))
        dq_t = jnp.zeros((LANES, wide), jnp.float32)
        for at in range(0, total, chunk):
            rows = slice(at, at + chunk)
            p = scores[rows, :] * jnp.exp2(tops[at // chunk] - log_norm)
            dp = dot_nt(values[rows, :], grads)
            ds = (p * (dp - delta)).astype(jnp.bfloat16)
            dv_acc[rows, :] += dot_nn(p.astype(jnp.bfloat16), grads)
            dk_acc[rows, :] += dot_nn(ds, queries)
            dq_t = dq_t + dot_nn(keys_t[:, rows], ds)
        dq_part[step, :, :] = dq_t

    tp = lax.axis_index("tp")
    for out, base, which in (
        (minus, 0, tp),
        (plus, 0, 1 - tp),
        (keep, half, tp),
        (send8, half, 1 - tp),
    ):
        for slot in range(HEADS):
            rows = pl.ds(pl.multiple_of(base + slot * ROWS + which * (ROWS // 2), ROWS // 2), ROWS // 2)
            out[slot, 0 : ROWS // 2, :] = (dk_acc[rows, :] * scale).astype(jnp.bfloat16)
            out[slot, ROWS // 2 : ROWS, :] = dv_acc[rows, :].astype(jnp.bfloat16)


def prefix_kernel(
    chunk, own, far1, far2, far3, pref, norms, dq_part,
    pgrad, dq,
    keys, values, keys_t, dk_acc, dv_acc, bulk,
):
    scale = 1.0 / math.sqrt(LANES)
    n_sib = pref.shape[0]
    pre = n_sib * 32
    gather_bulk(bulk, own, far1, far2, far3)
    load_keys(pref, keys, values)
    transpose_keys(keys, keys_t, 0, pre, chunk)
    dk_acc[...] = jnp.zeros_like(dk_acc)
    dv_acc[...] = jnp.zeros_like(dv_acc)

    @pl.loop(0, HEADS)
    def _(step):
        queries, grads, delta = tile_data(bulk, step)
        norm = norms[step][0:1]
        dq_t = dq_part[step]
        for at in range(0, pre, chunk):
            rows = slice(at, at + chunk)
            p = jnp.exp2(dot_nt(keys[rows, :], queries) * (scale * LOG2E) - norm)
            dp = dot_nt(values[rows, :], grads)
            ds = (p * (dp - delta)).astype(jnp.bfloat16)
            dv_acc[rows, :] += dot_nn(p.astype(jnp.bfloat16), grads)
            dk_acc[rows, :] += dot_nn(ds, queries)
            dq_t = dq_t + dot_nn(keys_t[:, rows], ds)
        dq[step, :, :] = (dq_t.T * scale).astype(jnp.bfloat16)

    for part in range(2):
        rows = slice(part * pre // 2, (part + 1) * pre // 2)
        pgrad[:, part * 32 : part * 32 + 16, :] = (
            (dk_acc[rows, :] * scale).astype(jnp.bfloat16).reshape(n_sib, 16, LANES)
        )
        pgrad[:, part * 32 + 16 : part * 32 + 32, :] = (
            dv_acc[rows, :].astype(jnp.bfloat16).reshape(n_sib, 16, LANES)
        )


def near_kernel(keep, got_plus, got_minus, out):
    for slot in range(HEADS):
        out[slot] = sum(a[slot].astype(jnp.float32) for a in (keep, got_plus, got_minus))


def merge_kernel(near, got8, dq, out0, out1, out2, out3):
    cq = lax.axis_index("cq")
    wide = GROUPS * ROWS
    for step, out in enumerate((out0, out1, out2, out3)):
        slot = jnp.bitwise_xor(cq, step)
        out[0:wide, :] = dq[step]
        total = near[slot] + got8[slot].astype(jnp.float32)
        out[wide : wide + ROWS, :] = total.astype(jnp.bfloat16)


def prefix_sum_kernel(parts, out):
    total = jnp.sum(parts[...].astype(jnp.float32), axis=0)
    for part in range(2):
        for piece in range(2 * HEADS):
            at = part * 32 + piece * 2
            rows = jnp.concatenate(
                [total[at : at + 2], total[at + 16 : at + 18], jnp.zeros((4, LANES), jnp.float32)],
                axis=0,
            )
            out[part * 2 * HEADS + piece, :, :] = rows


def unpack_kernel(back0, back1, back2, back3, small, dq_out, sk_out, sv_out, pk_out, pv_out):
    cq = lax.axis_index("cq")
    half = ROWS // 2
    wide = GROUPS * ROWS
    for step, back in enumerate((back0, back1, back2, back3)):
        head = jnp.bitwise_xor(cq, step)
        cols = pl.ds(pl.multiple_of(head * LANES, LANES), LANES)
        for slot in range(GROUPS):
            dq_out[slot, :, cols] = back[slot * ROWS : (slot + 1) * ROWS, :]
        sk_out[:, cols] = back[wide : wide + half, :]
        sv_out[:, cols] = back[wide + half : wide + ROWS, :]
    for head in range(HEADS):
        cols = slice(head * LANES, (head + 1) * LANES)
        total = sum(small[(b * HEADS + head) * 2 + t] for b in range(2) for t in range(2))
        pk_out[:, cols] = total[0:2].astype(jnp.bfloat16)
        pv_out[:, cols] = total[2:4].astype(jnp.bfloat16)


def ring_index(position):
    return (position % 8) * 2 + position // 8


def ring(shift, sources=range(16)):
    return [(ring_index(p), ring_index((p + shift) % 16)) for p in sources]


def on_device(n_sib, queries, gradient, forward, sib_k, sib_v, pre_k, pre_v, lengths):
    bf16 = jnp.bfloat16
    shape = jax.ShapeDtypeStruct

    pre = pl.pallas_call(
        pack_prefix_kernel,
        out_shape=shape((2 * HEADS, 16, LANES), bf16),
        in_specs=vmem(2),
        out_specs=vmem(1)[0],
        cost_estimate=cost(1 << 10, 1 << 16),
        name="pack_prefix",
    )(pre_k, pre_v)
    bulk = pl.pallas_call(
        pack_kernel,
        out_shape=(shape((784, LANES), bf16),) * 4,
        in_specs=[pl.BlockSpec(memory_space=pltpu.SMEM)]
        + vmem(5)
        + [pl.BlockSpec(memory_space=pl.ANY)],
        out_specs=tuple(vmem(4)),
        cost_estimate=cost(PACK_COST, 2 << 20),
        name="pack_heads",
    )(lengths, queries[0], gradient[0], forward[0], sib_k[0], sib_v[0], pre)

    def swap(array, step):
        return lax.ppermute(array, "cq", [(i, i ^ step) for i in range(HEADS)])

    bulk = [bulk[0]] + [swap(bulk[d], d) for d in (1, 2, 3)]
    pre = lax.all_to_all(pre, ("cb", "cq"), 0, 0)
    early = [p for p in range(16) if p % 8 < 4]
    pairs = [a[4 * ROWS : 6 * ROWS] for a in bulk]
    oth_lo = lax.ppermute(jnp.stack(pairs[0:2]), Z, ring(4, early))
    oth_hi = lax.ppermute(jnp.stack(pairs[2:4]), Z, ring(-4, early))
    spread = pl.pallas_call(
        spread_kernel,
        out_shape=shape((n_sib, 64, LANES), bf16),
        in_specs=vmem(1),
        out_specs=vmem(1)[0],
        cost_estimate=cost(SPREAD_COST, 1 << 19),
        name="spread_prefix",
    )(pre)
    pref = lax.all_to_all(spread, "sib", 0, 0)

    chunk = min(512, n_sib * 16)
    pre_rows, sib_rows = 32 * n_sib, 2 * HEADS * ROWS
    wide = GROUPS * ROWS
    norm_rows = shape((HEADS, 8, wide), jnp.float32)
    pre_norms = pl.pallas_call(
        functools.partial(norms_kernel, chunk),
        out_shape=norm_rows,
        in_specs=vmem(5),
        out_specs=vmem(1)[0],
        scratch_shapes=[
            pltpu.VMEM((pre_rows, LANES), bf16),
            pltpu.VMEM((HEADS, 784, LANES), bf16),
        ],
        compiler_params=pltpu.CompilerParams(vmem_limit_bytes=32 << 20),
        cost_estimate=cost(NORMS_COST, 1 << 20, HEADS * wide * 1024),
        name="prefix_norms",
    )(*bulk, pref)
    piece = shape((HEADS, ROWS, LANES), bf16)
    keep, send8, plus, minus, norms, dq_part = pl.pallas_call(
        functools.partial(sibling_kernel, chunk),
        out_shape=(piece,) * 4 + (norm_rows, shape((HEADS, LANES, wide), jnp.float32)),
        in_specs=vmem(7),
        out_specs=tuple(vmem(6)),
        scratch_shapes=[
            pltpu.VMEM((sib_rows, LANES), bf16),
            pltpu.VMEM((sib_rows, LANES), bf16),
            pltpu.VMEM((LANES, sib_rows), bf16),
            pltpu.VMEM((sib_rows, wide), jnp.float32),
            pltpu.VMEM((sib_rows, LANES), jnp.float32),
            pltpu.VMEM((sib_rows, LANES), jnp.float32),
            pltpu.VMEM((HEADS, 784, LANES), bf16),
        ],
        compiler_params=pltpu.CompilerParams(vmem_limit_bytes=32 << 20),
        cost_estimate=cost(10 * HEADS * wide * 1024 * LANES, 4 << 20, HEADS * wide * 1024),
        name="sibling_grads",
    )(*bulk, oth_lo, oth_hi, pre_norms)
    late = [p for p in range(16) if p % 8 >= 4]
    got8 = lax.ppermute(send8, Z, ring(8))
    got_plus = lax.ppermute(plus, Z, ring(4, late))
    got_minus = lax.ppermute(minus, Z, ring(-4, late))

    pgrad, dq = pl.pallas_call(
        functools.partial(prefix_kernel, chunk),
        out_shape=(shape((n_sib, 64, LANES), bf16), shape((HEADS, wide, LANES), bf16)),
        in_specs=vmem(7),
        out_specs=tuple(vmem(2)),
        scratch_shapes=[
            pltpu.VMEM((pre_rows, LANES), bf16),
            pltpu.VMEM((pre_rows, LANES), bf16),
            pltpu.VMEM((LANES, pre_rows), bf16),
            pltpu.VMEM((pre_rows, LANES), jnp.float32),
            pltpu.VMEM((pre_rows, LANES), jnp.float32),
            pltpu.VMEM((HEADS, 784, LANES), bf16),
        ],
        compiler_params=pltpu.CompilerParams(vmem_limit_bytes=32 << 20),
        cost_estimate=cost(GRADS_COST, 4 << 20, HEADS * wide * 1024),
        name="prefix_grads",
    )(*bulk, pref, norms, dq_part)

    parts = lax.all_to_all(pgrad, "sib", 0, 0)
    near = pl.pallas_call(
        near_kernel,
        out_shape=shape((HEADS, ROWS, LANES), jnp.float32),
        in_specs=vmem(3),
        out_specs=vmem(1)[0],
        cost_estimate=cost(MERGE_COST, 1 << 20),
        name="near_sums",
    )(keep, got_plus, got_minus)
    parts, near = lax.optimization_barrier((parts, near))
    back = pl.pallas_call(
        merge_kernel,
        out_shape=(shape((wide + ROWS, LANES), bf16),) * 4,
        in_specs=vmem(3),
        out_specs=tuple(vmem(4)),
        cost_estimate=cost(MERGE_COST, 1 << 20),
        name="merge_grads",
    )(near, got8, dq)
    small = pl.pallas_call(
        prefix_sum_kernel,
        out_shape=shape((16, 8, LANES), jnp.float32),
        in_specs=vmem(1),
        out_specs=vmem(1)[0],
        cost_estimate=cost(1 << 18, 1 << 19),
        name="prefix_sums",
    )(parts)
    small = lax.all_to_all(small, Z, 0, 0)
    back = [back[0]] + [swap(back[d], d) for d in (1, 2, 3)]

    dq_out, sk_out, sv_out, pk_out, pv_out = pl.pallas_call(
        unpack_kernel,
        out_shape=(
            shape((GROUPS, ROWS, HEADS * LANES), bf16),
            shape((ROWS // 2, HEADS * LANES), bf16),
            shape((ROWS // 2, HEADS * LANES), bf16),
            shape((2, HEADS * LANES), bf16),
            shape((2, HEADS * LANES), bf16),
        ),
        in_specs=vmem(5),
        out_specs=tuple(vmem(5)),
        cost_estimate=cost(1 << 18, 1 << 20),
        name="unpack_heads",
    )(*back, small)
    return dq_out[None], sk_out[None], sv_out[None], pk_out, pv_out


def solution(mesh):
    n_sib, n_ctx, n_tp = mesh.shape["sib"], mesh.shape["ctx"], mesh.shape["tp"]
    fine = Mesh(
        mesh.devices.reshape(n_sib, n_ctx // HEADS, HEADS, n_tp), ("sib", "cb", "cq", "tp")
    )
    ctx = ("cb", "cq")
    heads = P("sib", "tp", ctx, None)
    return jax.shard_map(
        functools.partial(on_device, n_sib),
        mesh=fine,
        in_specs=(
            heads,
            heads,
            heads,
            P("sib", ctx, None),
            P("sib", ctx, None),
            P(("sib",) + ctx, None),
            P(("sib",) + ctx, None),
            P(),
        ),
        out_specs=(
            heads,
            P("sib", ctx + ("tp",), None),
            P("sib", ctx + ("tp",), None),
            P(("sib",) + ctx + ("tp",), None),
            P(("sib",) + ctx + ("tp",), None),
        ),
        check_vma=False,
    )
```

```python
import functools
import math

import jax
import jax.numpy as jnp
from jax import lax
from jax.experimental import pallas as pl
from jax.experimental.pallas import tpu as pltpu
from jax.sharding import Mesh, PartitionSpec as P

HEADS = 4
LANES = 128
ROWS = 128
GROUPS = 2
LOG2E = math.log2(math.e)
NEG = -1e30
Z = ("cb", "cq", "tp")
NORMS_COST = 1 << 33
PACK_COST = 1 << 33
GRADS_COST = 1 << 36
MERGE_COST = 1 << 36
SPREAD_COST = 1 << 18


def dot_nt(a, b):
    return lax.dot_general(a, b, (((1,), (1,)), ((), ())), preferred_element_type=jnp.float32)


def dot_nn(a, b):
    return lax.dot_general(a, b, (((1,), (0,)), ((), ())), preferred_element_type=jnp.float32)


def vmem(n):
    return [pl.BlockSpec(memory_space=pltpu.VMEM)] * n


def cost(flops, moved, exps=0):
    return pl.CostEstimate(flops=flops, bytes_accessed=moved, transcendentals=exps)


def pack_kernel(lengths, q, g, o, k, v, pre, own, far1, far2, far3):
    cq = lax.axis_index("cq")
    ctx = lax.axis_index("cb") * HEADS + cq
    length = lengths[lax.axis_index("sib")]
    row = lax.broadcasted_iota(jnp.int32, (ROWS, LANES), 0) + ctx * ROWS
    live = row < length
    ones = jnp.ones((8, LANES), jnp.bfloat16)
    for step, out in enumerate((own, far1, far2, far3)):
        head = jnp.bitwise_xor(cq, step)
        cols = pl.ds(pl.multiple_of(head * LANES, LANES), LANES)
        out[4 * ROWS : 5 * ROWS, :] = k[:, cols]
        out[5 * ROWS : 6 * ROWS, :] = v[:, cols]
        deltas = []
        for slot in range(GROUPS):
            rows = slice(slot * ROWS, (slot + 1) * ROWS)
            out[rows, :] = q[slot, :, cols]
            grad = jnp.where(live, g[slot, :, cols].astype(jnp.float32), 0.0)
            rows = slice((GROUPS + slot) * ROWS, (GROUPS + slot + 1) * ROWS)
            out[rows, :] = grad.astype(jnp.bfloat16)
            prod = grad * o[slot, :, cols].astype(jnp.float32)
            high = prod.astype(jnp.bfloat16)
            low = (prod - high.astype(jnp.float32)).astype(jnp.bfloat16)
            deltas.append((dot_nt(ones, high) + dot_nt(ones, low))[0:1])
        rest = jnp.concatenate(deltas + [jnp.zeros((14, LANES), jnp.float32)], axis=0)
        out[6 * ROWS : 6 * ROWS + 16, :] = rest.astype(jnp.bfloat16)


def pack_prefix_kernel(pk, pv, pre):
    for head in range(HEADS):
        cols = slice(head * LANES, (head + 1) * LANES)
        rows = jnp.concatenate(
            [
                pk[:, cols].astype(jnp.float32),
                pv[:, cols].astype(jnp.float32),
                jnp.zeros((8, LANES), jnp.float32),
            ],
            axis=0,
        ).astype(jnp.bfloat16)
        for half in range(2):
            pre[half * HEADS + head] = rows


def spread_kernel(pre, out):
    rows = [pre[at].astype(jnp.float32) for at in range(2 * HEADS)]
    block = []
    for half in range(2):
        mine = rows[half * HEADS : (half + 1) * HEADS]
        block += [r[0:4] for r in mine] + [r[4:8] for r in mine]
    block = jnp.concatenate(block, axis=0).astype(jnp.bfloat16)
    for at in range(out.shape[0]):
        out[at] = block


def load_keys(pref, keys, values):
    pre = pref.shape[0] * 16
    for part in range(2):
        rows = slice(part * pre, (part + 1) * pre)
        keys[rows, :] = pref[:, part * 32 : part * 32 + 16, :].reshape(pre, LANES)
        values[rows, :] = pref[:, part * 32 + 16 : part * 32 + 32, :].reshape(pre, LANES)


def tile_data(bulk):
    wide = GROUPS * ROWS
    steps = range(HEADS)
    deltas = []
    for step in steps:
        rest = bulk[step][6 * ROWS : 6 * ROWS + 16, :].astype(jnp.float32)
        deltas += [rest[s : s + 1] for s in range(GROUPS)]
    queries = jnp.concatenate([bulk[step][0:wide, :] for step in steps], axis=0)
    grads = jnp.concatenate([bulk[step][wide : 2 * wide, :] for step in steps], axis=0)
    return queries, grads, jnp.concatenate(deltas, axis=1)


def transpose_keys(keys, keys_t, start, stop, chunk):
    for at in range(start, stop, chunk):
        keys_t[:, at - start : at - start + chunk] = (
            keys[at : at + chunk, :].astype(jnp.float32).T.astype(jnp.bfloat16)
        )


def load_sibling(bulk, oth_lo, oth_hi, keys, values, base):
    cq = lax.axis_index("cq")
    half = HEADS * ROWS
    for step in range(HEADS):
        at = jnp.bitwise_xor(cq, step) * ROWS
        src = (oth_lo if step < 2 else oth_hi).at[step % 2]
        rows = pl.ds(pl.multiple_of(base + at, ROWS), ROWS)
        keys[rows, :] = src[0:ROWS, :]
        if values is not None:
            values[rows, :] = src[ROWS : 2 * ROWS, :]
        rows = pl.ds(pl.multiple_of(base + half + at, ROWS), ROWS)
        keys[rows, :] = bulk[step][4 * ROWS : 5 * ROWS, :]
        if values is not None:
            values[rows, :] = bulk[step][5 * ROWS : 6 * ROWS, :]


def sibling_scores(keys, queries, at):
    half = HEADS * ROWS
    s = dot_nt(keys, queries) * (LOG2E / math.sqrt(LANES))
    if at >= half:
        cq = lax.axis_index("cq")
        lane = lax.broadcasted_iota(jnp.int32, (1, s.shape[1]), 1)
        tile = jnp.bitwise_xor(cq, lane // (GROUPS * ROWS))
        position = tile * ROWS + lax.rem(lane, ROWS)
        key_at = lax.broadcasted_iota(jnp.int32, s.shape, 0) + (at - half)
        return jnp.where(key_at <= position, s, NEG)
    return jnp.where(lax.axis_index("cb") == 1, s, NEG)


def norms_kernel(chunk, own, far1, far2, far3, pref, norms, keys):
    n_sib = pref.shape[0]
    pre = n_sib * 32
    wide = HEADS * GROUPS * ROWS
    bulk = (own, far1, far2, far3)
    for part in range(2):
        rows = slice(part * pre // 2, (part + 1) * pre // 2)
        keys[rows, :] = pref[:, part * 32 : part * 32 + 16, :].reshape(pre // 2, LANES)

    queries, grads, delta = tile_data(bulk)
    top = jnp.full((1, wide), NEG, jnp.float32)
    norm = jnp.zeros((1, wide), jnp.float32)
    for at in range(0, pre, chunk):
        s = dot_nt(keys[at : at + chunk, :], queries) * (LOG2E / math.sqrt(LANES))
        top, norm = online(s, top, norm)
    norms[...] = jnp.broadcast_to(top + jnp.log2(norm), (8, wide))


def online(s, top, norm):
    higher = jnp.maximum(top, jnp.max(s, axis=0, keepdims=True))
    added = jnp.sum(jnp.exp2(s - higher), axis=0, keepdims=True)
    return higher, norm * jnp.exp2(top - higher) + added


def sibling_kernel(
    chunk, own, far1, far2, far3, oth_lo, oth_hi, pre_norms,
    keep, send8, plus, minus, norms, dq_part,
    keys, values, keys_t, scores, dk_acc, dv_acc,
):
    scale = 1.0 / math.sqrt(LANES)
    total = keys.shape[0]
    half = HEADS * ROWS
    wide = HEADS * GROUPS * ROWS
    bulk = (own, far1, far2, far3)
    load_sibling(bulk, oth_lo, oth_hi, keys, values, 0)
    transpose_keys(keys, keys_t, 0, total, chunk)

    queries, grads, delta = tile_data(bulk)
    top = pre_norms[0:1]
    norm = jnp.ones((1, wide), jnp.float32)
    tops = []
    for at in range(0, total, chunk):
        s = sibling_scores(keys[at : at + chunk, :], queries, at)
        higher = jnp.maximum(top, jnp.max(s, axis=0, keepdims=True))
        e = jnp.exp2(s - higher)
        scores[at : at + chunk, :] = e
        norm = norm * jnp.exp2(top - higher) + jnp.sum(e, axis=0, keepdims=True)
        top = higher
        tops.append(top)
    log_norm = top + jnp.log2(norm)
    norms[...] = jnp.broadcast_to(log_norm, (8, wide))
    dq_t = jnp.zeros((LANES, wide), jnp.float32)
    for at in range(0, total, chunk):
        rows = slice(at, at + chunk)
        p = scores[rows, :] * jnp.exp2(tops[at // chunk] - log_norm)
        dp = dot_nt(values[rows, :], grads)
        ds = (p * (dp - delta)).astype(jnp.bfloat16)
        dv_acc[rows, :] = dot_nn(p.astype(jnp.bfloat16), grads)
        dk_acc[rows, :] = dot_nn(ds, queries)
        dq_t = dq_t + dot_nn(keys_t[:, rows], ds)
    dq_part[...] = dq_t

    tp = lax.axis_index("tp")
    for out, base, which in (
        (minus, 0, tp),
        (plus, 0, 1 - tp),
        (keep, half, tp),
        (send8, half, 1 - tp),
    ):
        for slot in range(HEADS):
            rows = pl.ds(pl.multiple_of(base + slot * ROWS + which * (ROWS // 2), ROWS // 2), ROWS // 2)
            out[slot, 0 : ROWS // 2, :] = (dk_acc[rows, :] * scale).astype(jnp.bfloat16)
            out[slot, ROWS // 2 : ROWS, :] = dv_acc[rows, :].astype(jnp.bfloat16)


def prefix_kernel(
    chunk, own, far1, far2, far3, pref, norms, dq_part,
    pgrad, dq,
    keys, values, keys_t, dk_acc, dv_acc,
):
    scale = 1.0 / math.sqrt(LANES)
    n_sib = pref.shape[0]
    pre = n_sib * 32
    bulk = (own, far1, far2, far3)
    load_keys(pref, keys, values)
    transpose_keys(keys, keys_t, 0, pre, chunk)

    queries, grads, delta = tile_data(bulk)
    norm = norms[0:1]
    dq_t = dq_part[...]
    for at in range(0, pre, chunk):
        rows = slice(at, at + chunk)
        p = jnp.exp2(dot_nt(keys[rows, :], queries) * (scale * LOG2E) - norm)
        dp = dot_nt(values[rows, :], grads)
        ds = (p * (dp - delta)).astype(jnp.bfloat16)
        dv_acc[rows, :] = dot_nn(p.astype(jnp.bfloat16), grads)
        dk_acc[rows, :] = dot_nn(ds, queries)
        dq_t = dq_t + dot_nn(keys_t[:, rows], ds)
    total = (dq_t.T * scale).astype(jnp.bfloat16)
    for step in range(HEADS):
        dq[step, :, :] = total[step * GROUPS * ROWS : (step + 1) * GROUPS * ROWS]

    for part in range(2):
        rows = slice(part * pre // 2, (part + 1) * pre // 2)
        pgrad[:, part * 32 : part * 32 + 16, :] = (
            (dk_acc[rows, :] * scale).astype(jnp.bfloat16).reshape(n_sib, 16, LANES)
        )
        pgrad[:, part * 32 + 16 : part * 32 + 32, :] = (
            dv_acc[rows, :].astype(jnp.bfloat16).reshape(n_sib, 16, LANES)
        )


def near_kernel(keep, got_plus, got_minus, out):
    for slot in range(HEADS):
        out[slot] = sum(a[slot].astype(jnp.float32) for a in (keep, got_plus, got_minus))


def merge_kernel(near, got8, dq, out0, out1, out2, out3):
    cq = lax.axis_index("cq")
    wide = GROUPS * ROWS
    for step, out in enumerate((out0, out1, out2, out3)):
        slot = jnp.bitwise_xor(cq, step)
        out[0:wide, :] = dq[step]
        total = near[slot] + got8[slot].astype(jnp.float32)
        out[wide : wide + ROWS, :] = total.astype(jnp.bfloat16)


def prefix_sum_kernel(parts, out):
    total = jnp.sum(parts[...].astype(jnp.float32), axis=0)
    for part in range(2):
        for piece in range(2 * HEADS):
            at = part * 32 + piece * 2
            rows = jnp.concatenate(
                [total[at : at + 2], total[at + 16 : at + 18], jnp.zeros((4, LANES), jnp.float32)],
                axis=0,
            )
            out[part * 2 * HEADS + piece, :, :] = rows


def unpack_kernel(back0, back1, back2, back3, small, dq_out, sk_out, sv_out, pk_out, pv_out):
    cq = lax.axis_index("cq")
    half = ROWS // 2
    wide = GROUPS * ROWS
    for step, back in enumerate((back0, back1, back2, back3)):
        head = jnp.bitwise_xor(cq, step)
        cols = pl.ds(pl.multiple_of(head * LANES, LANES), LANES)
        for slot in range(GROUPS):
            dq_out[slot, :, cols] = back[slot * ROWS : (slot + 1) * ROWS, :]
        sk_out[:, cols] = back[wide : wide + half, :]
        sv_out[:, cols] = back[wide + half : wide + ROWS, :]
    for head in range(HEADS):
        cols = slice(head * LANES, (head + 1) * LANES)
        total = sum(small[(b * HEADS + head) * 2 + t] for b in range(2) for t in range(2))
        pk_out[:, cols] = total[0:2].astype(jnp.bfloat16)
        pv_out[:, cols] = total[2:4].astype(jnp.bfloat16)


def ring_index(position):
    return (position % 8) * 2 + position // 8


def ring(shift, sources=range(16)):
    return [(ring_index(p), ring_index((p + shift) % 16)) for p in sources]


def on_device(n_sib, queries, gradient, forward, sib_k, sib_v, pre_k, pre_v, lengths):
    bf16 = jnp.bfloat16
    shape = jax.ShapeDtypeStruct

    pre = pl.pallas_call(
        pack_prefix_kernel,
        out_shape=shape((2 * HEADS, 16, LANES), bf16),
        in_specs=vmem(2),
        out_specs=vmem(1)[0],
        cost_estimate=cost(1 << 10, 1 << 16),
        name="pack_prefix",
    )(pre_k, pre_v)
    bulk = pl.pallas_call(
        pack_kernel,
        out_shape=(shape((784, LANES), bf16),) * 4,
        in_specs=[pl.BlockSpec(memory_space=pltpu.SMEM)]
        + vmem(5)
        + [pl.BlockSpec(memory_space=pl.ANY)],
        out_specs=tuple(vmem(4)),
        cost_estimate=cost(PACK_COST, 2 << 20),
        name="pack_heads",
    )(lengths, queries[0], gradient[0], forward[0], sib_k[0], sib_v[0], pre)

    def swap(array, step):
        return lax.ppermute(array, "cq", [(i, i ^ step) for i in range(HEADS)])

    bulk = [bulk[0]] + [swap(bulk[d], d) for d in (1, 2, 3)]
    pre = lax.all_to_all(pre, ("cb", "cq"), 0, 0)
    early = [p for p in range(16) if p % 8 < 4]
    pairs = [a[4 * ROWS : 6 * ROWS] for a in bulk]
    oth_lo = lax.ppermute(jnp.stack(pairs[0:2]), Z, ring(4, early))
    oth_hi = lax.ppermute(jnp.stack(pairs[2:4]), Z, ring(-4, early))
    spread = pl.pallas_call(
        spread_kernel,
        out_shape=shape((n_sib, 64, LANES), bf16),
        in_specs=vmem(1),
        out_specs=vmem(1)[0],
        cost_estimate=cost(SPREAD_COST, 1 << 19),
        name="spread_prefix",
    )(pre)
    pref = lax.all_to_all(spread, "sib", 0, 0)

    chunk = min(512, n_sib * 16)
    pre_rows, sib_rows = 32 * n_sib, 2 * HEADS * ROWS
    wide = GROUPS * ROWS
    norm_rows = shape((8, HEADS * wide), jnp.float32)
    pre_norms = pl.pallas_call(
        functools.partial(norms_kernel, min(512, n_sib * 32)),
        out_shape=norm_rows,
        in_specs=vmem(5),
        out_specs=vmem(1)[0],
        scratch_shapes=[
            pltpu.VMEM((pre_rows, LANES), bf16),
        ],
        compiler_params=pltpu.CompilerParams(vmem_limit_bytes=32 << 20),
        cost_estimate=cost(NORMS_COST, 1 << 20, HEADS * wide * 1024),
        name="prefix_norms",
    )(*bulk, pref)
    piece = shape((HEADS, ROWS, LANES), bf16)
    keep, send8, plus, minus, norms, dq_part = pl.pallas_call(
        functools.partial(sibling_kernel, chunk),
        out_shape=(piece,) * 4 + (norm_rows, shape((LANES, HEADS * wide), jnp.float32)),
        in_specs=vmem(7),
        out_specs=tuple(vmem(6)),
        scratch_shapes=[
            pltpu.VMEM((sib_rows, LANES), bf16),
            pltpu.VMEM((sib_rows, LANES), bf16),
            pltpu.VMEM((LANES, sib_rows), bf16),
            pltpu.VMEM((sib_rows, HEADS * wide), jnp.float32),
            pltpu.VMEM((sib_rows, LANES), jnp.float32),
            pltpu.VMEM((sib_rows, LANES), jnp.float32),
        ],
        compiler_params=pltpu.CompilerParams(vmem_limit_bytes=32 << 20),
        cost_estimate=cost(10 * HEADS * wide * 1024 * LANES, 4 << 20, HEADS * wide * 1024),
        name="sibling_grads",
    )(*bulk, oth_lo, oth_hi, pre_norms)
    late = [p for p in range(16) if p % 8 >= 4]
    got8 = lax.ppermute(send8, Z, ring(8))
    got_plus = lax.ppermute(plus, Z, ring(4, late))
    got_minus = lax.ppermute(minus, Z, ring(-4, late))

    pgrad, dq = pl.pallas_call(
        functools.partial(prefix_kernel, min(512, n_sib * 32)),
        out_shape=(shape((n_sib, 64, LANES), bf16), shape((HEADS, wide, LANES), bf16)),
        in_specs=vmem(7),
        out_specs=tuple(vmem(2)),
        scratch_shapes=[
            pltpu.VMEM((pre_rows, LANES), bf16),
            pltpu.VMEM((pre_rows, LANES), bf16),
            pltpu.VMEM((LANES, pre_rows), bf16),
            pltpu.VMEM((pre_rows, LANES), jnp.float32),
            pltpu.VMEM((pre_rows, LANES), jnp.float32),
        ],
        compiler_params=pltpu.CompilerParams(vmem_limit_bytes=32 << 20),
        cost_estimate=cost(GRADS_COST, 4 << 20, HEADS * wide * 1024),
        name="prefix_grads",
    )(*bulk, pref, norms, dq_part)

    parts = lax.all_to_all(pgrad, "sib", 0, 0)
    near = pl.pallas_call(
        near_kernel,
        out_shape=shape((HEADS, ROWS, LANES), jnp.float32),
        in_specs=vmem(3),
        out_specs=vmem(1)[0],
        cost_estimate=cost(MERGE_COST, 1 << 20),
        name="near_sums",
    )(keep, got_plus, got_minus)
    parts, near = lax.optimization_barrier((parts, near))
    back = pl.pallas_call(
        merge_kernel,
        out_shape=(shape((wide + ROWS, LANES), bf16),) * 4,
        in_specs=vmem(3),
        out_specs=tuple(vmem(4)),
        cost_estimate=cost(MERGE_COST, 1 << 20),
        name="merge_grads",
    )(near, got8, dq)
    small = pl.pallas_call(
        prefix_sum_kernel,
        out_shape=shape((16, 8, LANES), jnp.float32),
        in_specs=vmem(1),
        out_specs=vmem(1)[0],
        cost_estimate=cost(1 << 18, 1 << 19),
        name="prefix_sums",
    )(parts)
    small = lax.all_to_all(small, Z, 0, 0)
    back = [back[0]] + [swap(back[d], d) for d in (1, 2, 3)]

    dq_out, sk_out, sv_out, pk_out, pv_out = pl.pallas_call(
        unpack_kernel,
        out_shape=(
            shape((GROUPS, ROWS, HEADS * LANES), bf16),
            shape((ROWS // 2, HEADS * LANES), bf16),
            shape((ROWS // 2, HEADS * LANES), bf16),
            shape((2, HEADS * LANES), bf16),
            shape((2, HEADS * LANES), bf16),
        ),
        in_specs=vmem(5),
        out_specs=tuple(vmem(5)),
        cost_estimate=cost(1 << 18, 1 << 20),
        name="unpack_heads",
    )(*back, small)
    return dq_out[None], sk_out[None], sv_out[None], pk_out, pv_out


def solution(mesh):
    n_sib, n_ctx, n_tp = mesh.shape["sib"], mesh.shape["ctx"], mesh.shape["tp"]
    fine = Mesh(
        mesh.devices.reshape(n_sib, n_ctx // HEADS, HEADS, n_tp), ("sib", "cb", "cq", "tp")
    )
    ctx = ("cb", "cq")
    heads = P("sib", "tp", ctx, None)
    return jax.shard_map(
        functools.partial(on_device, n_sib),
        mesh=fine,
        in_specs=(
            heads,
            heads,
            heads,
            P("sib", ctx, None),
            P("sib", ctx, None),
            P(("sib",) + ctx, None),
            P(("sib",) + ctx, None),
            P(),
        ),
        out_specs=(
            heads,
            P("sib", ctx + ("tp",), None),
            P("sib", ctx + ("tp",), None),
            P(("sib",) + ctx + ("tp",), None),
            P(("sib",) + ctx + ("tp",), None),
        ),
        check_vma=False,
    )
```

```python
import functools
import math

import jax
import jax.numpy as jnp
from jax import lax
from jax.experimental import pallas as pl
from jax.experimental.pallas import tpu as pltpu
from jax.sharding import Mesh, PartitionSpec as P

HEADS = 4
LANES = 128
ROWS = 128
GROUPS = 2
LOG2E = math.log2(math.e)
NEG = -1e30
Z = ("cb", "cq", "tp")
NORMS_COST = 1 << 33
PACK_COST = 1 << 33
GRADS_COST = 1 << 36
MERGE_COST = 1 << 36
SPREAD_COST = 1 << 18


def dot_nt(a, b):
    return lax.dot_general(a, b, (((1,), (1,)), ((), ())), preferred_element_type=jnp.float32)


def dot_nn(a, b):
    return lax.dot_general(a, b, (((1,), (0,)), ((), ())), preferred_element_type=jnp.float32)


def vmem(n):
    return [pl.BlockSpec(memory_space=pltpu.VMEM)] * n


def cost(flops, moved, exps=0):
    return pl.CostEstimate(flops=flops, bytes_accessed=moved, transcendentals=exps)


def pack_kernel(lengths, q, g, o, k, v, pre, own, far1, far2, far3):
    cq = lax.axis_index("cq")
    ctx = lax.axis_index("cb") * HEADS + cq
    length = lengths[lax.axis_index("sib")]
    row = lax.broadcasted_iota(jnp.int32, (ROWS, LANES), 0) + ctx * ROWS
    live = row < length
    ones = jnp.ones((8, LANES), jnp.bfloat16)
    for step, out in enumerate((own, far1, far2, far3)):
        head = jnp.bitwise_xor(cq, step)
        cols = pl.ds(pl.multiple_of(head * LANES, LANES), LANES)
        out[4 * ROWS : 5 * ROWS, :] = k[:, cols]
        out[5 * ROWS : 6 * ROWS, :] = v[:, cols]
        deltas = []
        for slot in range(GROUPS):
            rows = slice(slot * ROWS, (slot + 1) * ROWS)
            out[rows, :] = q[slot, :, cols]
            grad = jnp.where(live, g[slot, :, cols].astype(jnp.float32), 0.0)
            rows = slice((GROUPS + slot) * ROWS, (GROUPS + slot + 1) * ROWS)
            out[rows, :] = grad.astype(jnp.bfloat16)
            prod = grad * o[slot, :, cols].astype(jnp.float32)
            high = prod.astype(jnp.bfloat16)
            low = (prod - high.astype(jnp.float32)).astype(jnp.bfloat16)
            deltas.append((dot_nt(ones, high) + dot_nt(ones, low))[0:1])
        rest = jnp.concatenate(deltas + [jnp.zeros((14, LANES), jnp.float32)], axis=0)
        out[6 * ROWS : 6 * ROWS + 16, :] = rest.astype(jnp.bfloat16)


def pack_prefix_kernel(pk, pv, pre):
    for head in range(HEADS):
        cols = slice(head * LANES, (head + 1) * LANES)
        rows = jnp.concatenate(
            [
                pk[:, cols].astype(jnp.float32),
                pv[:, cols].astype(jnp.float32),
                jnp.zeros((8, LANES), jnp.float32),
            ],
            axis=0,
        ).astype(jnp.bfloat16)
        for half in range(2):
            pre[half * HEADS + head] = rows


def spread_kernel(pre, out):
    rows = [pre[at].astype(jnp.float32) for at in range(2 * HEADS)]
    block = []
    for half in range(2):
        mine = rows[half * HEADS : (half + 1) * HEADS]
        block += [r[0:4] for r in mine] + [r[4:8] for r in mine]
    block = jnp.concatenate(block, axis=0).astype(jnp.bfloat16)
    for at in range(out.shape[0]):
        out[at] = block


def load_keys(pref, keys, values):
    pre = pref.shape[0] * 16
    for part in range(2):
        rows = slice(part * pre, (part + 1) * pre)
        keys[rows, :] = pref[:, part * 32 : part * 32 + 16, :].reshape(pre, LANES)
        values[rows, :] = pref[:, part * 32 + 16 : part * 32 + 32, :].reshape(pre, LANES)


def tile_data(bulk):
    wide = GROUPS * ROWS
    steps = range(HEADS)
    deltas = []
    for step in steps:
        rest = bulk[step][6 * ROWS : 6 * ROWS + 16, :].astype(jnp.float32)
        deltas += [rest[s : s + 1] for s in range(GROUPS)]
    queries = jnp.concatenate([bulk[step][0:wide, :] for step in steps], axis=0)
    grads = jnp.concatenate([bulk[step][wide : 2 * wide, :] for step in steps], axis=0)
    return queries, grads, jnp.concatenate(deltas, axis=1)


def transpose_keys(keys, keys_t, start, stop, chunk):
    for at in range(start, stop, chunk):
        keys_t[:, at - start : at - start + chunk] = (
            keys[at : at + chunk, :].astype(jnp.float32).T.astype(jnp.bfloat16)
        )


def load_sibling(bulk, oth_lo, oth_hi, keys, values, base):
    cq = lax.axis_index("cq")
    half = HEADS * ROWS
    for step in range(HEADS):
        at = jnp.bitwise_xor(cq, step) * ROWS
        src = (oth_lo if step < 2 else oth_hi).at[step % 2]
        rows = pl.ds(pl.multiple_of(base + at, ROWS), ROWS)
        keys[rows, :] = src[0:ROWS, :]
        if values is not None:
            values[rows, :] = src[ROWS : 2 * ROWS, :]
        rows = pl.ds(pl.multiple_of(base + half + at, ROWS), ROWS)
        keys[rows, :] = bulk[step][4 * ROWS : 5 * ROWS, :]
        if values is not None:
            values[rows, :] = bulk[step][5 * ROWS : 6 * ROWS, :]


def sibling_scores(keys, queries, at):
    half = HEADS * ROWS
    s = dot_nt(keys, queries) * (LOG2E / math.sqrt(LANES))
    if at >= half:
        cq = lax.axis_index("cq")
        lane = lax.broadcasted_iota(jnp.int32, (1, s.shape[1]), 1)
        tile = jnp.bitwise_xor(cq, lane // (GROUPS * ROWS))
        position = tile * ROWS + lax.rem(lane, ROWS)
        key_at = lax.broadcasted_iota(jnp.int32, s.shape, 0) + (at - half)
        return jnp.where(key_at <= position, s, NEG)
    return jnp.where(lax.axis_index("cb") == 1, s, NEG)


def norms_kernel(chunk, own, far1, far2, far3, pref, norms, keys):
    n_sib = pref.shape[0]
    pre = n_sib * 32
    wide = HEADS * GROUPS * ROWS
    bulk = (own, far1, far2, far3)
    for part in range(2):
        rows = slice(part * pre // 2, (part + 1) * pre // 2)
        keys[rows, :] = pref[:, part * 32 : part * 32 + 16, :].reshape(pre // 2, LANES)

    queries, grads, delta = tile_data(bulk)
    top = jnp.full((1, wide), NEG, jnp.float32)
    norm = jnp.zeros((1, wide), jnp.float32)
    for at in range(0, pre, chunk):
        s = dot_nt(keys[at : at + chunk, :], queries) * (LOG2E / math.sqrt(LANES))
        top, norm = online(s, top, norm)
    norms[...] = jnp.broadcast_to(top + jnp.log2(norm), (8, wide))


def online(s, top, norm):
    higher = jnp.maximum(top, jnp.max(s, axis=0, keepdims=True))
    added = jnp.sum(jnp.exp2(s - higher), axis=0, keepdims=True)
    return higher, norm * jnp.exp2(top - higher) + added


def sibling_kernel(
    chunk, own, far1, far2, far3, oth_lo, oth_hi, pre_norms,
    keep, send8, plus, minus, norms, dq_part,
    keys, values, keys_t, scores, dk_acc, dv_acc,
):
    scale = 1.0 / math.sqrt(LANES)
    total = keys.shape[0]
    half = HEADS * ROWS
    wide = HEADS * GROUPS * ROWS
    bulk = (own, far1, far2, far3)
    load_sibling(bulk, oth_lo, oth_hi, keys, values, 0)
    transpose_keys(keys, keys_t, 0, total, chunk)

    queries, grads, delta = tile_data(bulk)
    top = pre_norms[0:1]
    norm = jnp.ones((1, wide), jnp.float32)
    tops = []
    for at in range(0, total, chunk):
        s = sibling_scores(keys[at : at + chunk, :], queries, at)
        higher = jnp.maximum(top, jnp.max(s, axis=0, keepdims=True))
        e = jnp.exp2(s - higher)
        scores[at : at + chunk, :] = e
        norm = norm * jnp.exp2(top - higher) + jnp.sum(e, axis=0, keepdims=True)
        top = higher
        tops.append(top)
    log_norm = top + jnp.log2(norm)
    norms[...] = jnp.broadcast_to(log_norm, (8, wide))
    dq_t = jnp.zeros((LANES, wide), jnp.float32)
    for at in range(0, total, chunk):
        rows = slice(at, at + chunk)
        p = scores[rows, :] * jnp.exp2(tops[at // chunk] - log_norm)
        dp = dot_nt(values[rows, :], grads)
        ds = (p * (dp - delta)).astype(jnp.bfloat16)
        dv_acc[rows, :] = dot_nn(p.astype(jnp.bfloat16), grads)
        dk_acc[rows, :] = dot_nn(ds, queries)
        dq_t = dq_t + dot_nn(keys_t[:, rows], ds)
    dq_part[...] = dq_t

    tp = lax.axis_index("tp")
    for out, base, which in (
        (minus, 0, tp),
        (plus, 0, 1 - tp),
        (keep, half, tp),
        (send8, half, 1 - tp),
    ):
        for slot in range(HEADS):
            rows = pl.ds(pl.multiple_of(base + slot * ROWS + which * (ROWS // 2), ROWS // 2), ROWS // 2)
            out[slot, 0 : ROWS // 2, :] = (dk_acc[rows, :] * scale).astype(jnp.bfloat16)
            out[slot, ROWS // 2 : ROWS, :] = dv_acc[rows, :].astype(jnp.bfloat16)


def prefix_kernel(
    chunk, own, far1, far2, far3, pref, norms, dq_part,
    pgrad, dq,
    keys, values, keys_t, dk_acc, dv_acc,
):
    scale = 1.0 / math.sqrt(LANES)
    n_sib = pref.shape[0]
    pre = n_sib * 32
    bulk = (own, far1, far2, far3)
    load_keys(pref, keys, values)
    transpose_keys(keys, keys_t, 0, pre, chunk)

    queries, grads, delta = tile_data(bulk)
    norm = norms[0:1]
    dq_t = dq_part[...]
    for at in range(0, pre, chunk):
        rows = slice(at, at + chunk)
        p = jnp.exp2(dot_nt(keys[rows, :], queries) * (scale * LOG2E) - norm)
        dp = dot_nt(values[rows, :], grads)
        ds = (p * (dp - delta)).astype(jnp.bfloat16)
        dv_acc[rows, :] = dot_nn(p.astype(jnp.bfloat16), grads)
        dk_acc[rows, :] = dot_nn(ds, queries)
        dq_t = dq_t + dot_nn(keys_t[:, rows], ds)
    total = (dq_t.T * scale).astype(jnp.bfloat16)
    for step in range(HEADS):
        dq[step, :, :] = total[step * GROUPS * ROWS : (step + 1) * GROUPS * ROWS]

    for part in range(2):
        rows = slice(part * pre // 2, (part + 1) * pre // 2)
        pgrad[:, part * 32 : part * 32 + 16, :] = (
            (dk_acc[rows, :] * scale).astype(jnp.bfloat16).reshape(n_sib, 16, LANES)
        )
        pgrad[:, part * 32 + 16 : part * 32 + 32, :] = (
            dv_acc[rows, :].astype(jnp.bfloat16).reshape(n_sib, 16, LANES)
        )


def arrived_kernel(got_plus, got_minus, out):
    out[...] = jnp.zeros_like(out)


def merge_kernel(keep, got_plus, got_minus, got8, dq, out0, out1, out2, out3):
    cq = lax.axis_index("cq")
    wide = GROUPS * ROWS
    for step, out in enumerate((out0, out1, out2, out3)):
        slot = jnp.bitwise_xor(cq, step)
        out[0:wide, :] = dq[step]
        total = sum(a[slot].astype(jnp.float32) for a in (keep, got_plus, got_minus, got8))
        out[wide : wide + ROWS, :] = total.astype(jnp.bfloat16)


def prefix_sum_kernel(parts, arrived, out):
    total = jnp.sum(parts[...].astype(jnp.float32), axis=0)
    for part in range(2):
        for piece in range(2 * HEADS):
            at = part * 32 + piece * 2
            rows = jnp.concatenate(
                [total[at : at + 2], total[at + 16 : at + 18], jnp.zeros((4, LANES), jnp.float32)],
                axis=0,
            )
            out[part * 2 * HEADS + piece, :, :] = rows


def unpack_kernel(back0, back1, back2, back3, small, dq_out, sk_out, sv_out, pk_out, pv_out):
    cq = lax.axis_index("cq")
    half = ROWS // 2
    wide = GROUPS * ROWS
    for step, back in enumerate((back0, back1, back2, back3)):
        head = jnp.bitwise_xor(cq, step)
        cols = pl.ds(pl.multiple_of(head * LANES, LANES), LANES)
        for slot in range(GROUPS):
            dq_out[slot, :, cols] = back[slot * ROWS : (slot + 1) * ROWS, :]
        sk_out[:, cols] = back[wide : wide + half, :]
        sv_out[:, cols] = back[wide + half : wide + ROWS, :]
    for head in range(HEADS):
        cols = slice(head * LANES, (head + 1) * LANES)
        total = sum(small[(b * HEADS + head) * 2 + t] for b in range(2) for t in range(2))
        pk_out[:, cols] = total[0:2].astype(jnp.bfloat16)
        pv_out[:, cols] = total[2:4].astype(jnp.bfloat16)


def ring_index(position):
    return (position % 8) * 2 + position // 8


def ring(shift, sources=range(16)):
    return [(ring_index(p), ring_index((p + shift) % 16)) for p in sources]


def on_device(n_sib, queries, gradient, forward, sib_k, sib_v, pre_k, pre_v, lengths):
    bf16 = jnp.bfloat16
    shape = jax.ShapeDtypeStruct

    pre = pl.pallas_call(
        pack_prefix_kernel,
        out_shape=shape((2 * HEADS, 16, LANES), bf16),
        in_specs=vmem(2),
        out_specs=vmem(1)[0],
        cost_estimate=cost(1 << 10, 1 << 16),
        name="pack_prefix",
    )(pre_k, pre_v)
    bulk = pl.pallas_call(
        pack_kernel,
        out_shape=(shape((784, LANES), bf16),) * 4,
        in_specs=[pl.BlockSpec(memory_space=pltpu.SMEM)]
        + vmem(5)
        + [pl.BlockSpec(memory_space=pl.ANY)],
        out_specs=tuple(vmem(4)),
        cost_estimate=cost(PACK_COST, 2 << 20),
        name="pack_heads",
    )(lengths, queries[0], gradient[0], forward[0], sib_k[0], sib_v[0], pre)

    def swap(array, step):
        return lax.ppermute(array, "cq", [(i, i ^ step) for i in range(HEADS)])

    bulk = [bulk[0]] + [swap(bulk[d], d) for d in (1, 2, 3)]
    pre = lax.all_to_all(pre, ("cb", "cq"), 0, 0)
    early = [p for p in range(16) if p % 8 < 4]
    pairs = [a[4 * ROWS : 6 * ROWS] for a in bulk]
    oth_lo = lax.ppermute(jnp.stack(pairs[0:2]), Z, ring(4, early))
    oth_hi = lax.ppermute(jnp.stack(pairs[2:4]), Z, ring(-4, early))
    spread = pl.pallas_call(
        spread_kernel,
        out_shape=shape((n_sib, 64, LANES), bf16),
        in_specs=vmem(1),
        out_specs=vmem(1)[0],
        cost_estimate=cost(SPREAD_COST, 1 << 19),
        name="spread_prefix",
    )(pre)
    pref = lax.all_to_all(spread, "sib", 0, 0)

    chunk = min(512, n_sib * 16)
    pre_rows, sib_rows = 32 * n_sib, 2 * HEADS * ROWS
    wide = GROUPS * ROWS
    norm_rows = shape((8, HEADS * wide), jnp.float32)
    pre_norms = pl.pallas_call(
        functools.partial(norms_kernel, min(512, n_sib * 32)),
        out_shape=norm_rows,
        in_specs=vmem(5),
        out_specs=vmem(1)[0],
        scratch_shapes=[
            pltpu.VMEM((pre_rows, LANES), bf16),
        ],
        compiler_params=pltpu.CompilerParams(vmem_limit_bytes=32 << 20),
        cost_estimate=cost(NORMS_COST, 1 << 20, HEADS * wide * 1024),
        name="prefix_norms",
    )(*bulk, pref)
    piece = shape((HEADS, ROWS, LANES), bf16)
    keep, send8, plus, minus, norms, dq_part = pl.pallas_call(
        functools.partial(sibling_kernel, chunk),
        out_shape=(piece,) * 4 + (norm_rows, shape((LANES, HEADS * wide), jnp.float32)),
        in_specs=vmem(7),
        out_specs=tuple(vmem(6)),
        scratch_shapes=[
            pltpu.VMEM((sib_rows, LANES), bf16),
            pltpu.VMEM((sib_rows, LANES), bf16),
            pltpu.VMEM((LANES, sib_rows), bf16),
            pltpu.VMEM((sib_rows, HEADS * wide), jnp.float32),
            pltpu.VMEM((sib_rows, LANES), jnp.float32),
            pltpu.VMEM((sib_rows, LANES), jnp.float32),
        ],
        compiler_params=pltpu.CompilerParams(vmem_limit_bytes=32 << 20),
        cost_estimate=cost(10 * HEADS * wide * 1024 * LANES, 4 << 20, HEADS * wide * 1024),
        name="sibling_grads",
    )(*bulk, oth_lo, oth_hi, pre_norms)
    late = [p for p in range(16) if p % 8 >= 4]
    got8 = lax.ppermute(send8, Z, ring(8))
    got_plus = lax.ppermute(plus, Z, ring(4, late))
    got_minus = lax.ppermute(minus, Z, ring(-4, late))

    pgrad, dq = pl.pallas_call(
        functools.partial(prefix_kernel, min(512, n_sib * 32)),
        out_shape=(shape((n_sib, 64, LANES), bf16), shape((HEADS, wide, LANES), bf16)),
        in_specs=vmem(7),
        out_specs=tuple(vmem(2)),
        scratch_shapes=[
            pltpu.VMEM((pre_rows, LANES), bf16),
            pltpu.VMEM((pre_rows, LANES), bf16),
            pltpu.VMEM((LANES, pre_rows), bf16),
            pltpu.VMEM((pre_rows, LANES), jnp.float32),
            pltpu.VMEM((pre_rows, LANES), jnp.float32),
        ],
        compiler_params=pltpu.CompilerParams(vmem_limit_bytes=32 << 20),
        cost_estimate=cost(GRADS_COST, 4 << 20, HEADS * wide * 1024),
        name="prefix_grads",
    )(*bulk, pref, norms, dq_part)

    parts = lax.all_to_all(pgrad, "sib", 0, 0)
    arrived = pl.pallas_call(
        arrived_kernel,
        out_shape=shape((8, LANES), jnp.float32),
        in_specs=[pl.BlockSpec(memory_space=pl.ANY)] * 2,
        out_specs=vmem(1)[0],
        cost_estimate=cost(MERGE_COST, 1 << 10),
        name="arrived",
    )(got_plus, got_minus)
    parts, arrived, got_plus, got_minus = lax.optimization_barrier(
        (parts, arrived, got_plus, got_minus)
    )
    back = pl.pallas_call(
        merge_kernel,
        out_shape=(shape((wide + ROWS, LANES), bf16),) * 4,
        in_specs=vmem(5),
        out_specs=tuple(vmem(4)),
        cost_estimate=cost(MERGE_COST, 1 << 20),
        name="merge_grads",
    )(keep, got_plus, got_minus, got8, dq)
    small = pl.pallas_call(
        prefix_sum_kernel,
        out_shape=shape((16, 8, LANES), jnp.float32),
        in_specs=vmem(1) + [pl.BlockSpec(memory_space=pl.ANY)],
        out_specs=vmem(1)[0],
        cost_estimate=cost(1 << 18, 1 << 19),
        name="prefix_sums",
    )(parts, arrived)
    small = lax.all_to_all(small, Z, 0, 0)
    back = [back[0]] + [swap(back[d], d) for d in (1, 2, 3)]

    dq_out, sk_out, sv_out, pk_out, pv_out = pl.pallas_call(
        unpack_kernel,
        out_shape=(
            shape((GROUPS, ROWS, HEADS * LANES), bf16),
            shape((ROWS // 2, HEADS * LANES), bf16),
            shape((ROWS // 2, HEADS * LANES), bf16),
            shape((2, HEADS * LANES), bf16),
            shape((2, HEADS * LANES), bf16),
        ),
        in_specs=vmem(5),
        out_specs=tuple(vmem(5)),
        cost_estimate=cost(1 << 18, 1 << 20),
        name="unpack_heads",
    )(*back, small)
    return dq_out[None], sk_out[None], sv_out[None], pk_out, pv_out


def solution(mesh):
    n_sib, n_ctx, n_tp = mesh.shape["sib"], mesh.shape["ctx"], mesh.shape["tp"]
    fine = Mesh(
        mesh.devices.reshape(n_sib, n_ctx // HEADS, HEADS, n_tp), ("sib", "cb", "cq", "tp")
    )
    ctx = ("cb", "cq")
    heads = P("sib", "tp", ctx, None)
    return jax.shard_map(
        functools.partial(on_device, n_sib),
        mesh=fine,
        in_specs=(
            heads,
            heads,
            heads,
            P("sib", ctx, None),
            P("sib", ctx, None),
            P(("sib",) + ctx, None),
            P(("sib",) + ctx, None),
            P(),
        ),
        out_specs=(
            heads,
            P("sib", ctx + ("tp",), None),
            P("sib", ctx + ("tp",), None),
            P(("sib",) + ctx + ("tp",), None),
            P(("sib",) + ctx + ("tp",), None),
        ),
        check_vma=False,
    )
```

```python
import functools
import math

import jax
import jax.numpy as jnp
from jax import lax
from jax.experimental import pallas as pl
from jax.experimental.pallas import tpu as pltpu
from jax.sharding import Mesh, PartitionSpec as P

HEADS = 4
LANES = 128
ROWS = 128
GROUPS = 2
LOG2E = math.log2(math.e)
NEG = -1e30
Z = ("cb", "cq", "tp")
NORMS_COST = 1 << 33
PACK_COST = 1 << 33
GRADS_COST = 1 << 36
MERGE_COST = 1 << 36
SPREAD_COST = 1 << 18


def dot_nt(a, b):
    return lax.dot_general(a, b, (((1,), (1,)), ((), ())), preferred_element_type=jnp.float32)


def dot_nn(a, b):
    return lax.dot_general(a, b, (((1,), (0,)), ((), ())), preferred_element_type=jnp.float32)


def vmem(n):
    return [pl.BlockSpec(memory_space=pltpu.VMEM)] * n


def cost(flops, moved, exps=0):
    return pl.CostEstimate(flops=flops, bytes_accessed=moved, transcendentals=exps)


def pack_kernel(lengths, q, g, o, k, v, pre, own, far1, far2, far3):
    cq = lax.axis_index("cq")
    ctx = lax.axis_index("cb") * HEADS + cq
    length = lengths[lax.axis_index("sib")]
    row = lax.broadcasted_iota(jnp.int32, (ROWS, LANES), 0) + ctx * ROWS
    live = row < length
    ones = jnp.ones((8, LANES), jnp.bfloat16)
    for step, out in enumerate((own, far1, far2, far3)):
        head = jnp.bitwise_xor(cq, step)
        cols = pl.ds(pl.multiple_of(head * LANES, LANES), LANES)
        out[4 * ROWS : 5 * ROWS, :] = k[:, cols]
        out[5 * ROWS : 6 * ROWS, :] = v[:, cols]
        deltas = []
        for slot in range(GROUPS):
            rows = slice(slot * ROWS, (slot + 1) * ROWS)
            out[rows, :] = q[slot, :, cols]
            grad = jnp.where(live, g[slot, :, cols].astype(jnp.float32), 0.0)
            rows = slice((GROUPS + slot) * ROWS, (GROUPS + slot + 1) * ROWS)
            out[rows, :] = grad.astype(jnp.bfloat16)
            prod = grad * o[slot, :, cols].astype(jnp.float32)
            high = prod.astype(jnp.bfloat16)
            low = (prod - high.astype(jnp.float32)).astype(jnp.bfloat16)
            deltas.append((dot_nt(ones, high) + dot_nt(ones, low))[0:1])
        rest = jnp.concatenate(deltas + [jnp.zeros((14, LANES), jnp.float32)], axis=0)
        out[6 * ROWS : 6 * ROWS + 16, :] = rest.astype(jnp.bfloat16)


def pack_prefix_kernel(pk, pv, pre):
    for head in range(HEADS):
        cols = slice(head * LANES, (head + 1) * LANES)
        rows = jnp.concatenate(
            [
                pk[:, cols].astype(jnp.float32),
                pv[:, cols].astype(jnp.float32),
                jnp.zeros((8, LANES), jnp.float32),
            ],
            axis=0,
        ).astype(jnp.bfloat16)
        for half in range(2):
            pre[half * HEADS + head] = rows


def spread_kernel(pre, out):
    rows = [pre[at].astype(jnp.float32) for at in range(2 * HEADS)]
    block = []
    for half in range(2):
        mine = rows[half * HEADS : (half + 1) * HEADS]
        block += [r[0:4] for r in mine] + [r[4:8] for r in mine]
    block = jnp.concatenate(block, axis=0).astype(jnp.bfloat16)
    for at in range(out.shape[0]):
        out[at] = block


def load_keys(pref, keys, values):
    pre = pref.shape[0] * 16
    for part in range(2):
        rows = slice(part * pre, (part + 1) * pre)
        keys[rows, :] = pref[:, part * 32 : part * 32 + 16, :].reshape(pre, LANES)
        values[rows, :] = pref[:, part * 32 + 16 : part * 32 + 32, :].reshape(pre, LANES)


def tile_data(bulk):
    wide = GROUPS * ROWS
    steps = range(HEADS)
    deltas = []
    for step in steps:
        rest = bulk[step][6 * ROWS : 6 * ROWS + 16, :].astype(jnp.float32)
        deltas += [rest[s : s + 1] for s in range(GROUPS)]
    queries = jnp.concatenate([bulk[step][0:wide, :] for step in steps], axis=0)
    grads = jnp.concatenate([bulk[step][wide : 2 * wide, :] for step in steps], axis=0)
    return queries, grads, jnp.concatenate(deltas, axis=1)


def transpose_keys(keys, keys_t, start, stop, chunk):
    for at in range(start, stop, chunk):
        keys_t[:, at - start : at - start + chunk] = (
            keys[at : at + chunk, :].astype(jnp.float32).T.astype(jnp.bfloat16)
        )


def load_sibling(bulk, oth_lo, oth_hi, keys, values, base):
    cq = lax.axis_index("cq")
    half = HEADS * ROWS
    for step in range(HEADS):
        at = jnp.bitwise_xor(cq, step) * ROWS
        src = (oth_lo if step < 2 else oth_hi).at[step % 2]
        rows = pl.ds(pl.multiple_of(base + at, ROWS), ROWS)
        keys[rows, :] = src[0:ROWS, :]
        if values is not None:
            values[rows, :] = src[ROWS : 2 * ROWS, :]
        rows = pl.ds(pl.multiple_of(base + half + at, ROWS), ROWS)
        keys[rows, :] = bulk[step][4 * ROWS : 5 * ROWS, :]
        if values is not None:
            values[rows, :] = bulk[step][5 * ROWS : 6 * ROWS, :]


def sibling_scores(keys, queries, at):
    half = HEADS * ROWS
    s = dot_nt(keys, queries) * (LOG2E / math.sqrt(LANES))
    if at >= half:
        cq = lax.axis_index("cq")
        lane = lax.broadcasted_iota(jnp.int32, (1, s.shape[1]), 1)
        tile = jnp.bitwise_xor(cq, lane // (GROUPS * ROWS))
        position = tile * ROWS + lax.rem(lane, ROWS)
        key_at = lax.broadcasted_iota(jnp.int32, s.shape, 0) + (at - half)
        return jnp.where(key_at <= position, s, NEG)
    return jnp.where(lax.axis_index("cb") == 1, s, NEG)


def norms_kernel(chunk, own, far1, far2, far3, pref, norms, keys):
    n_sib = pref.shape[0]
    pre = n_sib * 32
    wide = HEADS * GROUPS * ROWS
    bulk = (own, far1, far2, far3)
    for part in range(2):
        rows = slice(part * pre // 2, (part + 1) * pre // 2)
        keys[rows, :] = pref[:, part * 32 : part * 32 + 16, :].reshape(pre // 2, LANES)

    queries, grads, delta = tile_data(bulk)
    top = jnp.full((1, wide), NEG, jnp.float32)
    norm = jnp.zeros((1, wide), jnp.float32)
    for at in range(0, pre, chunk):
        s = dot_nt(keys[at : at + chunk, :], queries) * (LOG2E / math.sqrt(LANES))
        top, norm = online(s, top, norm)
    norms[...] = jnp.broadcast_to(top + jnp.log2(norm), (8, wide))


def online(s, top, norm):
    higher = jnp.maximum(top, jnp.max(s, axis=0, keepdims=True))
    added = jnp.sum(jnp.exp2(s - higher), axis=0, keepdims=True)
    return higher, norm * jnp.exp2(top - higher) + added


def sibling_kernel(
    chunk, own, far1, far2, far3, oth_lo, oth_hi, pre_norms,
    keep, send8, plus, minus, norms, dq_part,
    keys, values, keys_t, scores, dk_acc, dv_acc,
):
    scale = 1.0 / math.sqrt(LANES)
    total = keys.shape[0]
    half = HEADS * ROWS
    wide = HEADS * GROUPS * ROWS
    bulk = (own, far1, far2, far3)
    load_sibling(bulk, oth_lo, oth_hi, keys, values, 0)
    transpose_keys(keys, keys_t, 0, total, chunk)

    queries, grads, delta = tile_data(bulk)
    top = pre_norms[0:1]
    norm = jnp.ones((1, wide), jnp.float32)
    tops = []
    for at in range(0, total, chunk):
        s = sibling_scores(keys[at : at + chunk, :], queries, at)
        higher = jnp.maximum(top, jnp.max(s, axis=0, keepdims=True))
        e = jnp.exp2(s - higher)
        scores[at : at + chunk, :] = e
        norm = norm * jnp.exp2(top - higher) + jnp.sum(e, axis=0, keepdims=True)
        top = higher
        tops.append(top)
    log_norm = top + jnp.log2(norm)
    norms[...] = jnp.broadcast_to(log_norm, (8, wide))
    dq_t = jnp.zeros((LANES, wide), jnp.float32)
    for at in range(0, total, chunk):
        rows = slice(at, at + chunk)
        p = scores[rows, :] * jnp.exp2(tops[at // chunk] - log_norm)
        dp = dot_nt(values[rows, :], grads)
        ds = (p * (dp - delta)).astype(jnp.bfloat16)
        dv_acc[rows, :] = dot_nn(p.astype(jnp.bfloat16), grads)
        dk_acc[rows, :] = dot_nn(ds, queries)
        dq_t = dq_t + dot_nn(keys_t[:, rows], ds)
    dq_part[...] = dq_t

    tp = lax.axis_index("tp")
    for out, base, which in (
        (minus, 0, tp),
        (plus, 0, 1 - tp),
        (keep, half, tp),
        (send8, half, 1 - tp),
    ):
        for slot in range(HEADS):
            rows = pl.ds(pl.multiple_of(base + slot * ROWS + which * (ROWS // 2), ROWS // 2), ROWS // 2)
            out[slot, 0 : ROWS // 2, :] = (dk_acc[rows, :] * scale).astype(jnp.bfloat16)
            out[slot, ROWS // 2 : ROWS, :] = dv_acc[rows, :].astype(jnp.bfloat16)


def prefix_kernel(
    chunk, own, far1, far2, far3, pref, norms, dq_part,
    pgrad, msg0, msg1, msg2, msg3,
    keys, values, keys_t, dk_acc, dv_acc,
):
    scale = 1.0 / math.sqrt(LANES)
    n_sib = pref.shape[0]
    pre = n_sib * 32
    bulk = (own, far1, far2, far3)
    load_keys(pref, keys, values)
    transpose_keys(keys, keys_t, 0, pre, chunk)

    queries, grads, delta = tile_data(bulk)
    norm = norms[0:1]
    dq_t = dq_part[...]
    for at in range(0, pre, chunk):
        rows = slice(at, at + chunk)
        p = jnp.exp2(dot_nt(keys[rows, :], queries) * (scale * LOG2E) - norm)
        dp = dot_nt(values[rows, :], grads)
        ds = (p * (dp - delta)).astype(jnp.bfloat16)
        dv_acc[rows, :] = dot_nn(p.astype(jnp.bfloat16), grads)
        dk_acc[rows, :] = dot_nn(ds, queries)
        dq_t = dq_t + dot_nn(keys_t[:, rows], ds)
    total = (dq_t.T * scale).astype(jnp.bfloat16)
    for step, msg in enumerate((msg0, msg1, msg2, msg3)):
        msg[0 : GROUPS * ROWS, :] = total[step * GROUPS * ROWS : (step + 1) * GROUPS * ROWS]

    for part in range(2):
        rows = slice(part * pre // 2, (part + 1) * pre // 2)
        pgrad[:, part * 32 : part * 32 + 16, :] = (
            (dk_acc[rows, :] * scale).astype(jnp.bfloat16).reshape(n_sib, 16, LANES)
        )
        pgrad[:, part * 32 + 16 : part * 32 + 32, :] = (
            dv_acc[rows, :].astype(jnp.bfloat16).reshape(n_sib, 16, LANES)
        )


def arrived_kernel(got_plus, got_minus, out):
    out[...] = jnp.zeros_like(out)


def merge_kernel(keep, got_plus, got_minus, got8, m0, m1, m2, m3, out0, out1, out2, out3):
    cq = lax.axis_index("cq")
    for step, out in enumerate((out0, out1, out2, out3)):
        slot = jnp.bitwise_xor(cq, step)
        total = sum(a[slot].astype(jnp.float32) for a in (keep, got_plus, got_minus, got8))
        out[...] = total.astype(jnp.bfloat16)


def prefix_sum_kernel(parts, arrived, out):
    total = jnp.sum(parts[...].astype(jnp.float32), axis=0)
    for part in range(2):
        for piece in range(2 * HEADS):
            at = part * 32 + piece * 2
            rows = jnp.concatenate(
                [total[at : at + 2], total[at + 16 : at + 18], jnp.zeros((4, LANES), jnp.float32)],
                axis=0,
            )
            out[part * 2 * HEADS + piece, :, :] = rows


def unpack_kernel(back0, back1, back2, back3, small, dq_out, sk_out, sv_out, pk_out, pv_out):
    cq = lax.axis_index("cq")
    half = ROWS // 2
    wide = GROUPS * ROWS
    for step, back in enumerate((back0, back1, back2, back3)):
        head = jnp.bitwise_xor(cq, step)
        cols = pl.ds(pl.multiple_of(head * LANES, LANES), LANES)
        for slot in range(GROUPS):
            dq_out[slot, :, cols] = back[slot * ROWS : (slot + 1) * ROWS, :]
        sk_out[:, cols] = back[wide : wide + half, :]
        sv_out[:, cols] = back[wide + half : wide + ROWS, :]
    for head in range(HEADS):
        cols = slice(head * LANES, (head + 1) * LANES)
        total = sum(small[(b * HEADS + head) * 2 + t] for b in range(2) for t in range(2))
        pk_out[:, cols] = total[0:2].astype(jnp.bfloat16)
        pv_out[:, cols] = total[2:4].astype(jnp.bfloat16)


def ring_index(position):
    return (position % 8) * 2 + position // 8


def ring(shift, sources=range(16)):
    return [(ring_index(p), ring_index((p + shift) % 16)) for p in sources]


def on_device(n_sib, queries, gradient, forward, sib_k, sib_v, pre_k, pre_v, lengths):
    bf16 = jnp.bfloat16
    shape = jax.ShapeDtypeStruct

    pre = pl.pallas_call(
        pack_prefix_kernel,
        out_shape=shape((2 * HEADS, 16, LANES), bf16),
        in_specs=vmem(2),
        out_specs=vmem(1)[0],
        cost_estimate=cost(1 << 10, 1 << 16),
        name="pack_prefix",
    )(pre_k, pre_v)
    bulk = pl.pallas_call(
        pack_kernel,
        out_shape=(shape((784, LANES), bf16),) * 4,
        in_specs=[pl.BlockSpec(memory_space=pltpu.SMEM)]
        + vmem(5)
        + [pl.BlockSpec(memory_space=pl.ANY)],
        out_specs=tuple(vmem(4)),
        cost_estimate=cost(PACK_COST, 2 << 20),
        name="pack_heads",
    )(lengths, queries[0], gradient[0], forward[0], sib_k[0], sib_v[0], pre)

    def swap(array, step):
        return lax.ppermute(array, "cq", [(i, i ^ step) for i in range(HEADS)])

    bulk = [bulk[0]] + [swap(bulk[d], d) for d in (1, 2, 3)]
    pre = lax.all_to_all(pre, ("cb", "cq"), 0, 0)
    early = [p for p in range(16) if p % 8 < 4]
    pairs = [a[4 * ROWS : 6 * ROWS] for a in bulk]
    oth_lo = lax.ppermute(jnp.stack(pairs[0:2]), Z, ring(4, early))
    oth_hi = lax.ppermute(jnp.stack(pairs[2:4]), Z, ring(-4, early))
    spread = pl.pallas_call(
        spread_kernel,
        out_shape=shape((n_sib, 64, LANES), bf16),
        in_specs=vmem(1),
        out_specs=vmem(1)[0],
        cost_estimate=cost(SPREAD_COST, 1 << 19),
        name="spread_prefix",
    )(pre)
    pref = lax.all_to_all(spread, "sib", 0, 0)

    chunk = min(512, n_sib * 16)
    pre_rows, sib_rows = 32 * n_sib, 2 * HEADS * ROWS
    wide = GROUPS * ROWS
    norm_rows = shape((8, HEADS * wide), jnp.float32)
    pre_norms = pl.pallas_call(
        functools.partial(norms_kernel, min(512, n_sib * 32)),
        out_shape=norm_rows,
        in_specs=vmem(5),
        out_specs=vmem(1)[0],
        scratch_shapes=[
            pltpu.VMEM((pre_rows, LANES), bf16),
        ],
        compiler_params=pltpu.CompilerParams(vmem_limit_bytes=32 << 20),
        cost_estimate=cost(NORMS_COST, 1 << 20, HEADS * wide * 1024),
        name="prefix_norms",
    )(*bulk, pref)
    piece = shape((HEADS, ROWS, LANES), bf16)
    keep, send8, plus, minus, norms, dq_part = pl.pallas_call(
        functools.partial(sibling_kernel, chunk),
        out_shape=(piece,) * 4 + (norm_rows, shape((LANES, HEADS * wide), jnp.float32)),
        in_specs=vmem(7),
        out_specs=tuple(vmem(6)),
        scratch_shapes=[
            pltpu.VMEM((sib_rows, LANES), bf16),
            pltpu.VMEM((sib_rows, LANES), bf16),
            pltpu.VMEM((LANES, sib_rows), bf16),
            pltpu.VMEM((sib_rows, HEADS * wide), jnp.float32),
            pltpu.VMEM((sib_rows, LANES), jnp.float32),
            pltpu.VMEM((sib_rows, LANES), jnp.float32),
        ],
        compiler_params=pltpu.CompilerParams(vmem_limit_bytes=32 << 20),
        cost_estimate=cost(10 * HEADS * wide * 1024 * LANES, 4 << 20, HEADS * wide * 1024),
        name="sibling_grads",
    )(*bulk, oth_lo, oth_hi, pre_norms)
    late = [p for p in range(16) if p % 8 >= 4]
    got8 = lax.ppermute(send8, Z, ring(8))
    got_plus = lax.ppermute(plus, Z, ring(4, late))
    got_minus = lax.ppermute(minus, Z, ring(-4, late))

    pgrad, *msgs = pl.pallas_call(
        functools.partial(prefix_kernel, min(512, n_sib * 32)),
        out_shape=(shape((n_sib, 64, LANES), bf16),) + (shape((wide + ROWS, LANES), bf16),) * 4,
        in_specs=vmem(7),
        out_specs=tuple(vmem(5)),
        scratch_shapes=[
            pltpu.VMEM((pre_rows, LANES), bf16),
            pltpu.VMEM((pre_rows, LANES), bf16),
            pltpu.VMEM((LANES, pre_rows), bf16),
            pltpu.VMEM((pre_rows, LANES), jnp.float32),
            pltpu.VMEM((pre_rows, LANES), jnp.float32),
        ],
        compiler_params=pltpu.CompilerParams(vmem_limit_bytes=32 << 20),
        cost_estimate=cost(GRADS_COST, 4 << 20, HEADS * wide * 1024),
        name="prefix_grads",
    )(*bulk, pref, norms, dq_part)

    parts = lax.all_to_all(pgrad, "sib", 0, 0)
    arrived = pl.pallas_call(
        arrived_kernel,
        out_shape=shape((8, LANES), jnp.float32),
        in_specs=[pl.BlockSpec(memory_space=pl.ANY)] * 2,
        out_specs=vmem(1)[0],
        cost_estimate=cost(MERGE_COST, 1 << 10),
        name="arrived",
    )(got_plus, got_minus)
    parts, arrived, got_plus, got_minus = lax.optimization_barrier(
        (parts, arrived, got_plus, got_minus)
    )
    back = pl.pallas_call(
        merge_kernel,
        out_shape=(shape((wide + ROWS, LANES), bf16),) * 4,
        grid=(1,),
        in_specs=[pl.BlockSpec((HEADS, ROWS, LANES), lambda i: (0, 0, 0))] * 4
        + [pl.BlockSpec(memory_space=pl.ANY)] * 4,
        out_specs=(pl.BlockSpec((ROWS, LANES), lambda i: (wide // ROWS, 0)),) * 4,
        input_output_aliases={4: 0, 5: 1, 6: 2, 7: 3},
        cost_estimate=cost(MERGE_COST, 1 << 20),
        name="merge_grads",
    )(keep, got_plus, got_minus, got8, *msgs)
    small = pl.pallas_call(
        prefix_sum_kernel,
        out_shape=shape((16, 8, LANES), jnp.float32),
        in_specs=vmem(1) + [pl.BlockSpec(memory_space=pl.ANY)],
        out_specs=vmem(1)[0],
        cost_estimate=cost(1 << 18, 1 << 19),
        name="prefix_sums",
    )(parts, arrived)
    small = lax.all_to_all(small, Z, 0, 0)
    back = [back[0]] + [swap(back[d], d) for d in (1, 2, 3)]

    dq_out, sk_out, sv_out, pk_out, pv_out = pl.pallas_call(
        unpack_kernel,
        out_shape=(
            shape((GROUPS, ROWS, HEADS * LANES), bf16),
            shape((ROWS // 2, HEADS * LANES), bf16),
            shape((ROWS // 2, HEADS * LANES), bf16),
            shape((2, HEADS * LANES), bf16),
            shape((2, HEADS * LANES), bf16),
        ),
        in_specs=vmem(5),
        out_specs=tuple(vmem(5)),
        cost_estimate=cost(1 << 18, 1 << 20),
        name="unpack_heads",
    )(*back, small)
    return dq_out[None], sk_out[None], sv_out[None], pk_out, pv_out


def solution(mesh):
    n_sib, n_ctx, n_tp = mesh.shape["sib"], mesh.shape["ctx"], mesh.shape["tp"]
    fine = Mesh(
        mesh.devices.reshape(n_sib, n_ctx // HEADS, HEADS, n_tp), ("sib", "cb", "cq", "tp")
    )
    ctx = ("cb", "cq")
    heads = P("sib", "tp", ctx, None)
    return jax.shard_map(
        functools.partial(on_device, n_sib),
        mesh=fine,
        in_specs=(
            heads,
            heads,
            heads,
            P("sib", ctx, None),
            P("sib", ctx, None),
            P(("sib",) + ctx, None),
            P(("sib",) + ctx, None),
            P(),
        ),
        out_specs=(
            heads,
            P("sib", ctx + ("tp",), None),
            P("sib", ctx + ("tp",), None),
            P(("sib",) + ctx + ("tp",), None),
            P(("sib",) + ctx + ("tp",), None),
        ),
        check_vma=False,
    )
```
